32 devices in a mesh: dp: 8 (over z, y), seq: 4 (over x, core).
Axes of the slice: x: 2, y: 2, z: 4, core: 2. Of those that a mesh axis runs over, the one named last changes fastest.
Arguments:
- patches: bfloat16 [8192, 768], P(('dp', 'seq')), may hold values from -6 to 6
- image_lengths: int32 [8, 3], P('dp'), may hold values from 193 to 576, as said below
- expert_ids: int32 [8192, 2], P(('dp', 'seq')), may hold values from 0 to 31, all different within a row; in each aligned block of 256 rows (0 to 255, 256 to 511, ...) at most 17 rows name the same one
- lower_norm_gain: float32 [768], P(('dp', 'seq')), may hold values from 0.5 to 1.5
- lower_norm_shift: float32 [768], P(('dp', 'seq')), may hold values from -1.25 to 1.25
- lower_project: float32 [768, 2304], P(('dp', 'seq')), may hold values from -0.21875 to 0.21875
- lower_query_bias: float32 [768], P(('dp', 'seq')), may hold values from -1.25 to 1.25
- lower_value_bias: float32 [768], P(('dp', 'seq')), may hold values from -1.25 to 1.25
- lower_merge: float32 [768, 768], P(('dp', 'seq')), may hold values from -1.75 to 1.75
- lower_merge_bias: float32 [768], P(('dp', 'seq')), may hold values from -1.25 to 1.25
- lower_second_gain: float32 [768], P(('dp', 'seq')), may hold values from 0.5 to 1.5
- lower_second_shift: float32 [768], P(('dp', 'seq')), may hold values from -1.25 to 1.25
- lower_expand: float32 [768, 3072], P(('dp', 'seq')), may hold values from -0.21875 to 0.21875
- lower_expand_bias: float32 [3072], P(('dp', 'seq')), may hold values from -1.25 to 1.25
- lower_shrink: float32 [3072, 768], P(('dp', 'seq')), may hold values from -0.109375 to 0.109375
- lower_shrink_bias: float32 [768], P(('dp', 'seq')), may hold values from -1.25 to 1.25
- upper_norm_gain: float32 [768], P(('dp', 'seq')), may hold values from 0.5 to 1.5
- upper_norm_shift: float32 [768], P(('dp', 'seq')), may hold values from -1.25 to 1.25
- upper_project: float32 [768, 2304], P(('dp', 'seq')), may hold values from -0.21875 to 0.21875
- upper_query_bias: float32 [768], P(('dp', 'seq')), may hold values from -1.25 to 1.25
- upper_value_bias: float32 [768], P(('dp', 'seq')), may hold values from -1.25 to 1.25
- upper_merge: float32 [768, 768], P(('dp', 'seq')), may hold values from -1.75 to 1.75
- upper_merge_bias: float32 [768], P(('dp', 'seq')), may hold values from -6 to 6
- upper_second_gain: float32 [768], P(('dp', 'seq')), may hold values from 0.5 to 1.5
- upper_second_shift: float32 [768], P(('dp', 'seq')), may hold values from -1.25 to 1.25
- router: float32 [768, 32], P(('dp', 'seq')), may hold values from -0.15625 to 0.15625
- expert_expand: float32 [768, 98304], P('seq', 'dp'), may hold values from -0.21875 to 0.21875
- expert_expand_bias: float32 [98304], P(('dp', 'seq')), may hold values from -1.25 to 1.25
- expert_shrink: float32 [98304, 768], P('dp', 'seq'), may hold values from -1.25 to 1.25
- expert_shrink_bias: float32 [32, 768], P(None, ('dp', 'seq')), may hold values from -3 to 3
- output_grad: float32 [8192, 768], P(('dp', 'seq')), may hold values from -6 to 6
Outputs:
- result: float32 [8192, 768], P(('dp', 'seq'))
- delta_patches: float32 [8192, 768], P(('dp', 'seq'))
- delta_lower_norm_gain: float32 [768], P(('dp', 'seq'))
- delta_lower_norm_shift: float32 [768], P(('dp', 'seq'))
- delta_lower_project: float32 [768, 2304], P(('dp', 'seq'))
- delta_lower_query_bias: float32 [768], P(('dp', 'seq'))
- delta_lower_value_bias: float32 [768], P(('dp', 'seq'))
- delta_lower_merge: float32 [768, 768], P(('dp', 'seq'))
- delta_lower_merge_bias: float32 [768], P(('dp', 'seq'))
- delta_lower_second_gain: float32 [768], P(('dp', 'seq'))
- delta_lower_second_shift: float32 [768], P(('dp', 'seq'))
- delta_lower_expand: float32 [768, 3072], P(('dp', 'seq'))
- delta_lower_expand_bias: float32 [3072], P(('dp', 'seq'))
- delta_lower_shrink: float32 [3072, 768], P(('dp', 'seq'))
- delta_lower_shrink_bias: float32 [768], P(('dp', 'seq'))
- delta_upper_norm_gain: float32 [768], P(('dp', 'seq'))
- delta_upper_norm_shift: float32 [768], P(('dp', 'seq'))
- delta_upper_project: float32 [768, 2304], P(('dp', 'seq'))
- delta_upper_query_bias: float32 [768], P(('dp', 'seq'))
- delta_upper_value_bias: float32 [768], P(('dp', 'seq'))
- delta_upper_merge: float32 [768, 768], P(('dp', 'seq'))
- delta_upper_merge_bias: float32 [768], P(('dp', 'seq'))
- delta_upper_second_gain: float32 [768], P(('dp', 'seq'))
- delta_upper_second_shift: float32 [768], P(('dp', 'seq'))
- delta_router: float32 [768, 32], P(('dp', 'seq'))
- delta_expert_expand: float32 [768, 98304], P('seq', 'dp')
- delta_expert_expand_bias: float32 [98304], P(('dp', 'seq'))
- delta_expert_shrink: float32 [98304, 768], P('dp', 'seq')
- delta_expert_shrink_bias: float32 [32, 768], P(None, ('dp', 'seq'))
The draws below stay inside these ranges and needn't reach their ends.
Inputs may be any that keep to these rules, and one draw needn't show every extreme that they name: `image_lengths`: row g gives the patch counts of group g's three images, laid end to end in this order over the group's 1024 patches; they sum to 1024, and the second one has exactly 576 patches and holds patches of all 4 parts of the group. `expert_ids`: each row names 2 different experts. In the rows of one device (aligned blocks of 256 rows) no expert is named by more than 17 rows, a bound that some block reaches.
All inputs are finite; a program needn't handle non-finite values.
Results may differ from the reference program's by a relative error of at most 0.039.
Values may be sent and summed in bfloat16 or wider, within the bound.
No kernel may reach another device: no remote copies, remote signals or barrier semaphores. Data moves between devices by JAX's collectives and lax.ppermute only.
A program may use at most 216 MiB of HBM per device.

```python
import math
import jax
import jax.numpy as jnp
import numpy as np
from jax import lax

D = 768
HEADS = 12
HEAD_DIM = 64
FF = 3072
E = 32
FFE = 3072
TOP = 2
TOK_DEV = 256
GROUP = 1024
GROUPS = 8
TOKENS = 8192
LONG = 576
CAP = 17
N_DP = 8
N_SEQ = 4


def draw_image_lengths(key, part):
    key = jax.random.fold_in(key, 7)
    lowest = 3 * TOK_DEV + 1 - LONG
    first_image = jax.random.randint(key, (GROUPS, 1), lowest, TOK_DEV, dtype=jnp.int32)
    middle_image = jnp.full((GROUPS, 1), LONG, dtype=jnp.int32)
    last_image = GROUP - LONG - first_image
    return jnp.concatenate([first_image, middle_image, last_image], axis=1)


def levels(own_key, shape, pieces, low, high):
    factor_of = 1.0
    for dim, blocks in pieces:
        heights = jax.random.uniform(jax.random.fold_in(jax.random.fold_in(own_key, 6), dim), (blocks,), jnp.float32, low / len(pieces), high / len(pieces))
        factor_of = factor_of * jnp.repeat(jnp.exp(heights), shape[dim] // blocks).reshape((-1,) + (1,) * (len(shape) - 1 - dim))
    return factor_of


def deal_out(rng, own, number, rows, number_of, top, reach, lean):
    order = jax.random.permutation(rng, number_of)
    crowded, usual = load_shares(number_of, rows * top, reach, lean, True), load_shares(number_of, rows * top, reach, lean, False)
    places = jnp.arange(number_of)

    def named(sizes, rotation):
        used = int((sizes > 0).sum())
        fixed = max(1, used // 4)
        shifted = fixed + (places - fixed + rotation * (used - fixed)) % max(1, number_of - fixed)
        return jnp.zeros((number_of,), jnp.int32).at[order[jnp.where(places < fixed, places, shifted)]].set(jnp.asarray(sizes, jnp.int32))

    sizes = jnp.where(number % 4 == 0, named(crowded, number // 4), named(usual, number - number // 4 - 1))
    mixed = jax.random.permutation(jax.random.fold_in(own, 3), number_of)
    donor, sink = mixed[0:number_of // 2 * 2:2], mixed[1:number_of // 2 * 2:2]
    margin = jnp.minimum(sizes[donor] - 1, reach - sizes[sink]) // 2
    margin = jnp.where((donor == order[0]) | (sink == order[0]) | (sizes[sink] == 0), 0, jnp.maximum(margin, 0))
    shifted = jax.random.randint(jax.random.fold_in(own, 4), (number_of // 2,), 0, 1 << 20) % (margin + 1)
    sizes = sizes.at[donor].add(-shifted).at[sink].add(shifted)
    members = jnp.searchsorted(jnp.cumsum(sizes), jnp.arange(rows * top), side="right").astype(jnp.int32)
    grid = members.reshape(top, rows).T
    grid = grid[jax.random.permutation(jax.random.fold_in(own, 1), rows)]
    rotation = jax.random.randint(jax.random.fold_in(own, 2), (rows, 1), 0, top)
    return jnp.take_along_axis(grid, (jnp.arange(top)[None, :] + rotation) % top, axis=1)


def load_shares(count, total, bound, skew, full):
    loads = [(1 << 20) // math.isqrt(grade ** skew) + 1 for grade in range(1, count + 1)]
    largest = bound if full else min(bound, max(-(-total // count), total * loads[0] // sum(loads)))
    least = 1 if total - largest >= count - 1 else 0
    holding, rest = [largest] + [least] * (count - 1), total - largest - least * (count - 1)
    while rest > 0:
        candidates = [i for i in range(1, count) if holding[i] < largest] or [i for i in range(1, count) if holding[i] < bound]
        pool, remaining = sum([loads[i] for i in candidates]), rest
        for i in candidates:
            extra = min(bound - holding[i], max(1, remaining * loads[i] // pool), rest)
            holding[i] = holding[i] + extra
            rest = rest - extra
    return np.array(holding)


def bell_draw(own_key, dims, scale, limit, pieces=(), held_as=jnp.bfloat16):
    factor_of = levels(own_key, dims, pieces, -0.22, 0.18) if pieces else 1.0
    values = jax.random.normal(own_key, dims, jnp.float32) * scale * factor_of
    return jnp.minimum(jnp.maximum(values, -limit), limit).astype(held_as)


def setup_inputs(seed: int = 0) -> dict:
    key_of = jax.random.split(jax.random.key(seed), 32)
    patches = bell_draw(key_of[0], (TOKENS, D), 1.0, 6.0, ((0, 32),))
    image_lengths = draw_image_lengths(jax.random.fold_in(key_of[31], 71), 0)
    expert_ids_keys = jax.random.split(jax.random.fold_in(key_of[2], 1), TOKENS // TOK_DEV)
    expert_ids_turns = jax.random.permutation(jax.random.fold_in(key_of[2], 3), TOKENS // TOK_DEV)
    expert_ids = jax.vmap(lambda own, number: deal_out(jax.random.fold_in(key_of[2], 2), own, number, TOK_DEV, E, TOP, CAP, 0))(expert_ids_keys, expert_ids_turns).reshape((TOKENS, TOP))
    lower_norm_gain = jnp.clip(1.0 + 0.1 * jax.random.normal(key_of[3], (D,), jnp.float32), 0.5, 1.5)
    lower_norm_shift = bell_draw(key_of[4], (D,), 0.2, 1.25, ((0, 32),), jnp.float32)
    lower_project = bell_draw(key_of[5], (D, 3 * D), D ** -0.5, 0.21875, ((0, 32),), jnp.float32)
    lower_query_bias = bell_draw(key_of[6], (D,), 0.2, 1.25, ((0, 32),), jnp.float32)
    lower_value_bias = bell_draw(key_of[7], (D,), 0.2, 1.25, ((0, 32),), jnp.float32)
    lower_merge = bell_draw(key_of[8], (D, D), (D // 64) ** -0.5, 1.75, ((0, 32),), jnp.float32)
    lower_merge_bias = bell_draw(key_of[9], (D,), 0.2, 1.25, ((0, 32),), jnp.float32)
    lower_second_gain = jnp.clip(1.0 + 0.1 * jax.random.normal(key_of[10], (D,), jnp.float32), 0.5, 1.5)
    lower_second_shift = bell_draw(key_of[11], (D,), 0.2, 1.25, ((0, 32),), jnp.float32)
    lower_expand = bell_draw(key_of[12], (D, FF), D ** -0.5, 0.21875, ((0, 32),), jnp.float32)
    lower_expand_bias = bell_draw(key_of[13], (FF,), 0.2, 1.25, ((0, 32),), jnp.float32)
    lower_shrink = bell_draw(key_of[14], (FF, D), FF ** -0.5, 0.109375, ((0, 32),), jnp.float32)
    lower_shrink_bias = bell_draw(key_of[15], (D,), 0.2, 1.25, ((0, 32),), jnp.float32)
    upper_norm_gain = jnp.clip(1.0 + 0.1 * jax.random.normal(key_of[16], (D,), jnp.float32), 0.5, 1.5)
    upper_norm_shift = bell_draw(key_of[17], (D,), 0.2, 1.25, ((0, 32),), jnp.float32)
    upper_project = bell_draw(key_of[18], (D, 3 * D), D ** -0.5, 0.21875, ((0, 32),), jnp.float32)
    upper_query_bias = bell_draw(key_of[19], (D,), 0.2, 1.25, ((0, 32),), jnp.float32)
    upper_value_bias = bell_draw(key_of[20], (D,), 0.2, 1.25, ((0, 32),), jnp.float32)
    upper_merge = bell_draw(key_of[21], (D, D), (D // 64) ** -0.5, 1.75, ((0, 32),), jnp.float32)
    upper_merge_bias = bell_draw(key_of[22], (D,), 1.0, 6.0, ((0, 32),), jnp.float32)
    upper_second_gain = jnp.clip(1.0 + 0.1 * jax.random.normal(key_of[23], (D,), jnp.float32), 0.5, 1.5)
    upper_second_shift = bell_draw(key_of[24], (D,), 0.2, 1.25, ((0, 32),), jnp.float32)
    router = bell_draw(key_of[25], (D, E), (2 * D) ** -0.5, 0.15625, ((0, 32),), jnp.float32)
    expert_expand = bell_draw(key_of[26], (D, E * FFE), D ** -0.5, 0.21875, ((0, 4), (1, 8)), jnp.float32)
    expert_expand_bias = bell_draw(key_of[27], (E * FFE,), 0.2, 1.25, ((0, 32),), jnp.float32)
    expert_shrink = bell_draw(key_of[28], (E * FFE, D), (max(FFE // 128, 1)) ** -0.5, 1.25, ((0, 8), (1, 4)), jnp.float32)
    expert_shrink_bias = bell_draw(key_of[29], (E, D), 0.5, 3.0, ((1, 32),), jnp.float32)
    output_grad = bell_draw(key_of[30], (TOKENS, D), 1.0, 6.0, ((0, 32),), jnp.float32)
    return {"patches": patches, "image_lengths": image_lengths, "expert_ids": expert_ids, "lower_norm_gain": lower_norm_gain, "lower_norm_shift": lower_norm_shift, "lower_project": lower_project, "lower_query_bias": lower_query_bias, "lower_value_bias": lower_value_bias, "lower_merge": lower_merge, "lower_merge_bias": lower_merge_bias, "lower_second_gain": lower_second_gain, "lower_second_shift": lower_second_shift, "lower_expand": lower_expand, "lower_expand_bias": lower_expand_bias, "lower_shrink": lower_shrink, "lower_shrink_bias": lower_shrink_bias, "upper_norm_gain": upper_norm_gain, "upper_norm_shift": upper_norm_shift, "upper_project": upper_project, "upper_query_bias": upper_query_bias, "upper_value_bias": upper_value_bias, "upper_merge": upper_merge, "upper_merge_bias": upper_merge_bias, "upper_second_gain": upper_second_gain, "upper_second_shift": upper_second_shift, "router": router, "expert_expand": expert_expand, "expert_expand_bias": expert_expand_bias, "expert_shrink": expert_shrink, "expert_shrink_bias": expert_shrink_bias, "output_grad": output_grad}


HIGH = lax.Precision.HIGHEST
MASKED = -1000000000.0
EPSILON = 1e-06

@jax.custom_vjp
def low(v):
    return lax.optimization_barrier(v.astype(jnp.bfloat16)).astype(jnp.float32)

@jax.custom_vjp
def low_back(v):
    return v

def low_keep(v):
    return (low(v), None)

def low_pass(kept, grad):
    return (grad,)

def back_keep(v):
    return (v, None)

def back_low(kept, grad):
    return (low(grad),)
low.defvjp(low_keep, low_pass)
low_back.defvjp(back_keep, back_low)

def layer_norm(inputs, gain, shift):
    center = inputs - lax.optimization_barrier(jnp.mean(inputs, axis=-1, keepdims=True))
    spread = lax.optimization_barrier(jnp.mean(center * center, axis=-1, keepdims=True))
    return center * lax.rsqrt(spread + EPSILON) * gain + shift

def product(left, right):
    return jnp.dot(left, right, precision=HIGH, preferred_element_type=jnp.float32)

def softmax_rows(scores):
    highest = lax.optimization_barrier(jnp.max(scores, axis=-1, keepdims=True))
    raised = jnp.exp(scores - highest)
    return raised / lax.optimization_barrier(jnp.sum(raised, axis=-1, keepdims=True))

def image_numbers(lengths, count):
    places = jnp.arange(count, dtype=jnp.int32)
    first_end = lengths[0]
    second_end = lengths[0] + lengths[1]
    return (places >= first_end).astype(jnp.int32) + (places >= second_end).astype(jnp.int32)

def attention_block(residual, numbers, weights):
    gain, shift, project, query_bias, value_bias, merge, merge_bias = weights
    length = residual.shape[0]
    normed = low(layer_norm(residual, low(gain), low(shift)))
    packed = product(normed, low(project))
    queries = low(low_back(packed[:, :D] + low(query_bias))).reshape(length, HEADS, HEAD_DIM)
    key_rows = low(low_back(packed[:, D:2 * D])).reshape(length, HEADS, HEAD_DIM)
    value_rows = low(low_back(packed[:, 2 * D:] + low(value_bias))).reshape(length, HEADS, HEAD_DIM)
    scale = 1.0 / HEAD_DIM ** 0.5
    scores = low_back(jnp.einsum('qhd,khd->hqk', queries, key_rows, precision=HIGH) * scale)
    same_image = numbers[:, None] == numbers[None, :]
    probs = softmax_rows(jnp.where(same_image[None], scores, MASKED))
    attended = jnp.einsum('hqk,khd->qhd', low(probs), value_rows, precision=HIGH).reshape(length, D)
    attended = low(low_back(attended))
    return residual + low_back(product(attended, low(merge)) + low(merge_bias))

def mlp_block(residual, weights):
    gain, shift, expand, expand_bias, shrink, shrink_bias = weights
    normed = low(layer_norm(residual, low(gain), low(shift)))
    before = low_back(product(normed, low(expand)) + low(expand_bias))
    hidden = low(jax.nn.gelu(before, approximate=False))
    return residual + low_back(product(hidden, low(shrink)) + low(shrink_bias))

def slot_places(expert_rows):
    parts = expert_rows.reshape(N_SEQ, TOK_DEV, TOP)
    chosen = (parts[:, :, :, None] == jnp.arange(E, dtype=jnp.int32)).astype(jnp.int32)
    per_row = lax.optimization_barrier(jnp.sum(chosen, axis=2))
    earlier = jnp.cumsum(per_row, axis=1) - per_row
    slots = lax.optimization_barrier(jnp.sum(chosen * earlier[:, :, None, :], axis=3))
    offsets = CAP * jnp.arange(N_SEQ, dtype=jnp.int32)
    return (slots + offsets[:, None, None]).reshape(N_SEQ * TOK_DEV, TOP)

def expert_block(residual, expert_rows, weights):
    gain, shift, router, expand, expand_bias, shrink, shrink_bias = weights
    length = residual.shape[0]
    normed = low(layer_norm(residual, low(gain), low(shift)))
    probs = softmax_rows(low_back(product(normed, low(router))))
    gating = jnp.take_along_axis(probs, expert_rows, axis=1)
    places = slot_places(expert_rows)
    repeated = jnp.broadcast_to(normed[:, None, :], (length, TOP, D))
    filled = jnp.zeros((E, N_SEQ * CAP, D), jnp.float32).at[expert_rows, places].set(repeated)
    before = low_back(jnp.einsum('ecd,def->ecf', filled, low(expand).reshape(D, E, FFE), precision=HIGH) + low(expand_bias).reshape(E, 1, FFE))
    hidden = low(jax.nn.gelu(before, approximate=False))
    outputs = low_back(jnp.einsum('ecf,efd->ecd', hidden, low(shrink).reshape(E, FFE, D), precision=HIGH) + low(shrink_bias)[:, None, :])
    picked = outputs[expert_rows, places]
    return residual + lax.optimization_barrier(jnp.sum(gating[:, :, None] * picked, axis=1))

def reference(patches, image_lengths, expert_ids, lower_norm_gain, lower_norm_shift, lower_project, lower_query_bias, lower_value_bias, lower_merge, lower_merge_bias, lower_second_gain, lower_second_shift, lower_expand, lower_expand_bias, lower_shrink, lower_shrink_bias, upper_norm_gain, upper_norm_shift, upper_project, upper_query_bias, upper_value_bias, upper_merge, upper_merge_bias, upper_second_gain, upper_second_shift, router, expert_expand, expert_expand_bias, expert_shrink, expert_shrink_bias, output_grad):
    params = (lower_norm_gain, lower_norm_shift, lower_project, lower_query_bias, lower_value_bias, lower_merge, lower_merge_bias, lower_second_gain, lower_second_shift, lower_expand, lower_expand_bias, lower_shrink, lower_shrink_bias, upper_norm_gain, upper_norm_shift, upper_project, upper_query_bias, upper_value_bias, upper_merge, upper_merge_bias, upper_second_gain, upper_second_shift, router, expert_expand, expert_expand_bias, expert_shrink, expert_shrink_bias)
    grouped_ids = expert_ids.reshape(N_DP, N_SEQ * TOK_DEV, TOP)

    def forward(inputs, weights):
        lower_attention = weights[0:7]
        lower_mlp = weights[7:13]
        upper_attention = weights[13:20]
        upper_expert = weights[20:27]

        def one_group(group):
            residual, lengths, expert_rows = group
            numbers = image_numbers(lengths, residual.shape[0])
            residual = attention_block(residual, numbers, lower_attention)
            residual = mlp_block(residual, lower_mlp)
            residual = attention_block(residual, numbers, upper_attention)
            return expert_block(residual, expert_rows, upper_expert)
        grouped = inputs.reshape(N_DP, N_SEQ * TOK_DEV, D)
        return lax.map(jax.checkpoint(one_group), (grouped, image_lengths, grouped_ids)).reshape(-1, D)
    result, pullback = jax.vjp(forward, patches.astype(jnp.float32), params)
    delta_inputs, deltas = pullback(output_grad.astype(jnp.float32))
    return (result, delta_inputs, deltas[0], deltas[1], deltas[2], deltas[3], deltas[4], deltas[5], deltas[6], deltas[7], deltas[8], deltas[9], deltas[10], deltas[11], deltas[12], deltas[13], deltas[14], deltas[15], deltas[16], deltas[17], deltas[18], deltas[19], deltas[20], deltas[21], deltas[22], deltas[23], deltas[24], deltas[25], deltas[26])
```

```python
import functools
import math

import jax
import jax.numpy as jnp
from jax import lax
from jax.experimental import pallas as pl
from jax.experimental.pallas import tpu as pltpu
from jax.sharding import Mesh
from jax.sharding import PartitionSpec as P

HEADS = 12
CAP = 17
LONG = 576
EDGE = 192
MASKED = -1000000000.0
EPSILON = 1e-06
LOWTYPE = jnp.bfloat16
WIDE = jnp.float32
ALL = ("z", "y", "x", "c")
CHIPS = ("z", "y", "x")
SWAP = [(0, 1), (1, 0)]


def dot(left, right, dims):
    return lax.dot_general(left, right, ((dims[0], dims[1]), ((), ())), preferred_element_type=WIDE)


def product(left, right):
    return dot(left, right, ((1,), (0,)))


def over_rows(left, right):
    return dot(left, right, ((0,), (0,)))


def over_features(left, right):
    return dot(left, right, ((1,), (1,)))


def low(values):
    return values.astype(LOWTYPE)


def widen(values):
    return values.astype(WIDE)


def swap_cores(values):
    return lax.ppermute(values, "c", SWAP)


def swap_chips(values):
    return lax.ppermute(values, "x", SWAP)


def in_order(mine, other, index, axis):
    first = jnp.where(index == 0, mine, other)
    second = jnp.where(index == 0, other, mine)
    return jnp.concatenate([first, second], axis=axis)


def norm_parts(values):
    center = values - jnp.mean(values, axis=-1, keepdims=True)
    spread = jnp.mean(center * center, axis=-1, keepdims=True)
    return center, lax.rsqrt(spread + EPSILON)


def layer_norm(values, gain, shift):
    center, scale = norm_parts(values)
    return low(center * scale * gain + shift)


def layer_norm_back(values, gain, grad):
    center, scale = norm_parts(values)
    hat = center * scale
    inner = grad * gain
    dvalues = scale * (
        inner
        - jnp.mean(inner, axis=-1, keepdims=True)
        - hat * jnp.mean(inner * hat, axis=-1, keepdims=True)
    )
    return dvalues, jnp.sum(grad * hat, axis=0), jnp.sum(grad, axis=0)


def gelu_parts(values):
    cdf = 0.5 + 0.5 * lax.erf(values * math.sqrt(0.5))
    pdf = jnp.exp(-0.5 * values * values) * (1.0 / math.sqrt(2.0 * math.pi))
    return values * cdf, cdf + values * pdf


def image_of(places, first_end, second_end):
    return (places >= first_end).astype(jnp.int32) + (places >= second_end).astype(jnp.int32)


def attention_places(scalars, rows, halo):
    x = scalars[0]
    edge_start = pl.multiple_of(x * (rows // 2), 64)
    mid_start = pl.multiple_of((1 - x) * (rows - halo), 64)
    mid_place = rows * x + mid_start
    halo_place = rows + x * ((rows - halo) - rows)
    return edge_start, mid_start, rows * x + edge_start, mid_place, halo_place


def edge_mask(place, count, first_end, second_end):
    row = image_of(place + lax.broadcasted_iota(jnp.int32, (count, 1), 0), first_end, second_end)
    column = image_of(place + lax.broadcasted_iota(jnp.int32, (1, count), 1), first_end, second_end)
    return (row == column) & (column != 1)


def mid_mask(mid_place, halo_place, count, first_end, second_end):
    row_places = mid_place + lax.broadcasted_iota(jnp.int32, (count, 1), 0)
    columns = lax.broadcasted_iota(jnp.int32, (1, 2 * count), 1)
    column_places = jnp.where(columns < count, mid_place + columns, halo_place + columns - count)
    row = image_of(row_places, first_end, second_end) == 1
    column = image_of(column_places, first_end, second_end) == 1
    return row & column, row


def lane_of_head(head, dim, lanes):
    lane = lax.broadcasted_iota(jnp.int32, (1, lanes), 1)
    return (lane >= head * dim) & (lane < (head + 1) * dim)


def only(values, lanes):
    return jnp.where(lanes, values, jnp.zeros_like(values))


def attend_kernel(scalars, packed, out, logs, *, rows, halo, dim):
    share = out.shape[1]
    first_end, second_end = scalars[1], scalars[2]
    edge_start, mid_start, edge_place, mid_place, halo_place = attention_places(scalars, rows, halo)
    half = rows // 2
    scale = 1.0 / math.sqrt(dim)
    mask_edge = edge_mask(edge_place, half, first_end, second_end)
    mask_mid, row_mid = mid_mask(mid_place, halo_place, halo, first_end, second_end)

    def one(queries, keys, values, mask):
        total, log_total = None, None
        for head in range(2):
            lanes = lane_of_head(head, dim, 128)
            scores = jnp.where(mask, over_features(only(queries, lanes), keys) * scale, MASKED)
            highest = jnp.max(scores, axis=-1, keepdims=True)
            raised = jnp.exp(scores - highest)
            sums = jnp.sum(raised, axis=-1, keepdims=True)
            weights = low(raised * (1.0 / sums))
            part = product(weights, only(values, lanes))
            total = part if total is None else total + part
            log_sum = highest + jnp.log(sums)
            log_total = log_sum if head == 0 else jnp.where(lanes, log_sum, log_total)
        return total, log_total

    def pair(index, carry):
        query_lanes = pl.ds(pl.multiple_of(index * 128, 128), 128)
        key_lanes = pl.ds(pl.multiple_of(share + index * 128, 128), 128)
        value_lanes = pl.ds(pl.multiple_of(2 * share + index * 128, 128), 128)
        edge = pl.ds(edge_start, half)
        mid = pl.ds(mid_start, halo)
        far = pl.ds(rows, halo)
        result, log_total = one(
            packed[edge, query_lanes], packed[edge, key_lanes], packed[edge, value_lanes], mask_edge
        )
        out[edge, query_lanes] = low(result)
        logs[edge, query_lanes] = log_total
        keys = jnp.concatenate([packed[mid, key_lanes], packed[far, key_lanes]], axis=0)
        values = jnp.concatenate([packed[mid, value_lanes], packed[far, value_lanes]], axis=0)
        result, log_total = one(packed[mid, query_lanes], keys, values, mask_mid)
        out[mid, query_lanes] = jnp.where(row_mid, low(result), out[mid, query_lanes])
        logs[mid, query_lanes] = jnp.where(row_mid, log_total, logs[mid, query_lanes])
        return carry

    lax.fori_loop(0, share // 128, pair, 0)


def attend_back_kernel(scalars, packed, grads, logs, out, *, rows, halo, dim):
    share = grads.shape[1]
    first_end, second_end = scalars[1], scalars[2]
    edge_start, mid_start, edge_place, mid_place, halo_place = attention_places(scalars, rows, halo)
    half = rows // 2
    scale = 1.0 / math.sqrt(dim)
    mask_edge = edge_mask(edge_place, half, first_end, second_end)
    mask_mid, _ = mid_mask(mid_place, halo_place, halo, first_end, second_end)

    def one(queries, keys, values, grad, log_total, mask):
        dquery, dkey, dvalue = None, None, None
        for head in range(2):
            lanes = lane_of_head(head, dim, 128)
            query, key, dout = only(queries, lanes), only(keys, lanes), only(grad, lanes)
            logs_here = log_total[:, head * dim : head * dim + 1]
            scores = jnp.where(mask, over_features(query, keys) * scale, MASKED)
            probs = jnp.exp(scores - logs_here)
            dprobs = over_features(dout, values)
            delta = jnp.sum(probs * dprobs, axis=-1, keepdims=True)
            dscores = low(probs * (dprobs - delta))
            parts = (
                product(dscores, key) * scale,
                over_rows(dscores, query) * scale,
                over_rows(low(probs), dout),
            )
            if head == 0:
                dquery, dkey, dvalue = parts
            else:
                dquery, dkey, dvalue = dquery + parts[0], dkey + parts[1], dvalue + parts[2]
        return low(dquery), low(dkey), low(dvalue)

    out[...] = jnp.zeros_like(out)

    def pair(index, carry):
        query_lanes = pl.ds(pl.multiple_of(index * 128, 128), 128)
        key_lanes = pl.ds(pl.multiple_of(share + index * 128, 128), 128)
        value_lanes = pl.ds(pl.multiple_of(2 * share + index * 128, 128), 128)
        edge = pl.ds(edge_start, half)
        mid = pl.ds(mid_start, halo)
        far = pl.ds(rows, halo)
        dquery, dkey, dvalue = one(
            packed[edge, query_lanes],
            packed[edge, key_lanes],
            packed[edge, value_lanes],
            grads[edge, query_lanes],
            logs[edge, query_lanes],
            mask_edge,
        )
        out[edge, query_lanes] = dquery
        out[edge, key_lanes] = dkey
        out[edge, value_lanes] = dvalue
        keys = jnp.concatenate([packed[mid, key_lanes], packed[far, key_lanes]], axis=0)
        values = jnp.concatenate([packed[mid, value_lanes], packed[far, value_lanes]], axis=0)
        dquery, dkey, dvalue = one(
            packed[mid, query_lanes],
            keys,
            values,
            grads[mid, query_lanes],
            logs[mid, query_lanes],
            mask_mid,
        )
        out[mid, query_lanes] = out[mid, query_lanes] + dquery
        out[mid, key_lanes] = out[mid, key_lanes] + dkey[:halo]
        out[mid, value_lanes] = out[mid, value_lanes] + dvalue[:halo]
        out[far, key_lanes] = dkey[halo:]
        out[far, value_lanes] = dvalue[halo:]
        return carry

    lax.fori_loop(0, share // 128, pair, 0)


def kernel_call(body, outs, operands, flops):
    return pl.pallas_call(
        body,
        out_shape=outs,
        in_specs=[pl.BlockSpec(memory_space=pltpu.SMEM)]
        + [pl.BlockSpec(memory_space=pltpu.VMEM)] * (len(operands) - 1),
        out_specs=[pl.BlockSpec(memory_space=pltpu.VMEM)] * len(outs),
        compiler_params=pltpu.CompilerParams(vmem_limit_bytes=48 * 1024 * 1024),
        cost_estimate=pl.CostEstimate(flops=flops, bytes_accessed=8_000_000, transcendentals=1_700_000),
    )(*operands)


def attend(scalars, packed, rows, halo, dim):
    share = packed.shape[1] // 3
    return kernel_call(
        functools.partial(attend_kernel, rows=rows, halo=halo, dim=dim),
        [jax.ShapeDtypeStruct((rows, share), LOWTYPE), jax.ShapeDtypeStruct((rows, share), WIDE)],
        [scalars, packed],
        1_700_000_000,
    )


def attend_back(scalars, packed, grads, logs, rows, halo, dim):
    [out] = kernel_call(
        functools.partial(attend_back_kernel, rows=rows, halo=halo, dim=dim),
        [jax.ShapeDtypeStruct(packed.shape, LOWTYPE)],
        [scalars, packed, grads, logs],
        4_000_000_000,
    )
    return out


def pick(block, index):
    return lax.dynamic_index_in_dim(block, index, 0, keepdims=False)


def gather_rows(block, core):
    pair = in_order(pick(block, core), swap_cores(pick(block, 1 - core)), core, 0)
    return lax.all_gather(pair, CHIPS, axis=0, tiled=True)


def scatter_rows(grads, core):
    summed = lax.psum_scatter(low(grads), CHIPS, scatter_dimension=0, tiled=True)
    parts = summed.reshape(2, summed.shape[0] // 2, summed.shape[1])
    mine, other = pick(parts, core), swap_cores(pick(parts, 1 - core))
    return mine, other


def thirds(weight, width):
    rows = weight.shape[0]
    return weight.reshape(rows, 3, 2, width // 2).transpose(2, 0, 1, 3).reshape(2, rows, -1)


def columns(weight):
    rows = weight.shape[0]
    return weight.reshape(rows, 2, -1).transpose(1, 0, 2)


def local(
    patches,
    image_lengths,
    expert_ids,
    lower_norm_gain,
    lower_norm_shift,
    lower_project,
    lower_query_bias,
    lower_value_bias,
    lower_merge,
    lower_merge_bias,
    lower_second_gain,
    lower_second_shift,
    lower_expand,
    lower_expand_bias,
    lower_shrink,
    lower_shrink_bias,
    upper_norm_gain,
    upper_norm_shift,
    upper_project,
    upper_query_bias,
    upper_value_bias,
    upper_merge,
    upper_merge_bias,
    upper_second_gain,
    upper_second_shift,
    router,
    expert_expand,
    expert_expand_bias,
    expert_shrink,
    expert_shrink_bias,
    output_grad,
):
    x, core = lax.axis_index("x"), lax.axis_index("c")
    devices = lax.axis_size(ALL)
    here = lax.axis_index(ALL)
    own, width = patches.shape
    rows = 2 * own
    dim = width // HEADS
    halo = rows - EDGE
    share = width // 2
    experts = router.shape[1]
    copies = devices // experts
    slots = experts * CAP
    part = lower_norm_gain.shape[0]
    hidden_part = lower_expand_bias.shape[0]
    lengths = image_lengths[0]
    scalars = jnp.stack([x, lengths[0], lengths[0] + lengths[1]]).astype(jnp.int32)
    mid_start = (1 - x) * (rows - halo)

    def halo_rows(full):
        count = halo // 2
        piece = lax.dynamic_slice_in_dim(full, mid_start + core * count, count, 0)
        got = swap_chips(piece)
        return in_order(got, swap_cores(got), core, 0)

    vectors = [
        lower_norm_gain,
        lower_norm_shift,
        lower_query_bias,
        lower_value_bias,
        lower_merge_bias,
        lower_second_gain,
        lower_second_shift,
        lower_shrink_bias,
        upper_norm_gain,
        upper_norm_shift,
        upper_query_bias,
        upper_value_bias,
        upper_merge_bias,
        upper_second_gain,
        upper_second_shift,
    ]
    count = len(vectors)
    small = jnp.concatenate(
        [
            jnp.stack(vectors, axis=1),
            lower_expand_bias.reshape(part, hidden_part // part),
            router,
            expert_shrink_bias.T,
        ],
        axis=1,
    )
    extra = hidden_part // part
    small = jnp.pad(small, ((0, 0), (0, 128 - small.shape[1])))
    small = jnp.broadcast_to(low(small)[None], (2, part, 128))
    first = gather_rows(
        jnp.concatenate(
            [thirds(low(lower_project), width), columns(low(lower_merge)), small], axis=2
        ),
        core,
    )
    lower_project_c = first[:, : 3 * share]
    lower_merge_c = first[:, 3 * share : 4 * share]
    lower_merge_full = in_order(lower_merge_c, swap_cores(lower_merge_c), core, 1)
    table = first[:, 4 * share :]
    table_t = widen(table.T)
    (
        ln1_gain,
        ln1_shift,
        lower_qb,
        lower_vb,
        lower_mb,
        ln2_gain,
        ln2_shift,
        shrink_b,
        ln3_gain,
        ln3_shift,
        upper_qb,
        upper_vb,
        upper_mb,
        ln4_gain,
        ln4_shift,
    ) = [table_t[i] for i in range(count)]
    expand_b = widen(table[:, count : count + extra]).reshape(devices, 2, hidden_part // 2)
    expand_b = lax.dynamic_index_in_dim(expand_b, core, 1, keepdims=False).reshape(-1)
    router_w = table[:, count + extra : count + extra + experts]
    router_t = table.T[count + extra : count + extra + experts]
    expert_bias = table.T[count + extra + experts : count + extra + 2 * experts]

    expand_c = gather_rows(
        low(lower_expand)
        .reshape(part, devices, 2, hidden_part // 2)
        .transpose(2, 0, 1, 3)
        .reshape(2, part, -1),
        core,
    )
    shrink_c = gather_rows(low(lower_shrink).reshape(2, hidden_part // 2, width), core)
    third = gather_rows(
        jnp.concatenate([thirds(low(upper_project), width), columns(low(upper_merge))], axis=2),
        core,
    )
    upper_project_c = third[:, : 3 * share]
    upper_merge_c = third[:, 3 * share :]
    upper_merge_full = in_order(upper_merge_c, swap_cores(upper_merge_c), core, 1)

    def whole_expert(weight):
        units = weight.shape[1] // 4
        pieces = low(weight).reshape(weight.shape[0], 4, units).transpose(1, 0, 2)
        return lax.all_to_all(pieces, ("x", "c"), 0, 0, tiled=True).reshape(-1, units)

    def expert_parts(grads):
        pieces = low(grads).reshape(4, grads.shape[0] // 4, grads.shape[1])
        pieces = lax.all_to_all(pieces, ("x", "c"), 0, 0, tiled=True)
        return widen(pieces.transpose(1, 0, 2).reshape(pieces.shape[1], -1))

    expand_e = whole_expert(expert_expand)
    shrink_e = whole_expert(expert_shrink.T)

    order = lax.broadcasted_iota(jnp.int32, (own, own), 0)
    before_it = low(order > lax.broadcasted_iota(jnp.int32, (own, own), 1))
    chosen = [
        low(expert_ids[:, k : k + 1] == jnp.arange(experts, dtype=jnp.int32)[None]) for k in range(2)
    ]
    earlier = product(before_it, chosen[0] + chosen[1])
    places = [
        expert_ids[:, k] * CAP
        + jnp.sum(widen(chosen[k]) * earlier, axis=1).astype(jnp.int32)
        for k in range(2)
    ]
    placed = [
        low(place[:, None] == jnp.arange(slots, dtype=jnp.int32)[None]) for place in places
    ]
    placed_any = placed[0] + placed[1]

    def to_experts(values):
        sent = low(over_rows(placed_any, values)).reshape(experts, CAP, width)
        if copies > 1:
            sent = jnp.repeat(sent, copies, axis=0)
        got = lax.all_to_all(sent, ALL, 0, 0, tiled=True)
        return got.reshape(devices * CAP, width)

    def to_patches(values):
        got = lax.all_to_all(low(values).reshape(devices, CAP, width), ALL, 0, 0, tiled=True)
        if copies > 1:
            got = low(jnp.sum(widen(got.reshape(experts, copies, CAP, width)), axis=1))
        return got.reshape(slots, width)

    grad_rows = to_experts(low(output_grad))

    full = in_order(patches, swap_cores(patches), core, 0)
    x0 = widen(full)

    def half(vector):
        return lax.dynamic_slice_in_dim(vector, core * share, share, 0)

    def attention_forward(residual, normed, project_c, query_bias, value_bias):
        bias = jnp.concatenate([half(query_bias), jnp.zeros((share,), WIDE), half(value_bias)])
        packed = low(product(normed, project_c) + bias)
        attended, logs = attend(scalars, packed, rows, halo, dim)
        attended_full = in_order(attended, swap_cores(attended), core, 1)
        return packed, logs, attended_full

    a1 = layer_norm(jnp.concatenate([x0, widen(halo_rows(full))], axis=0), ln1_gain, ln1_shift)
    packed1, logs1, attended1 = attention_forward(x0, a1, lower_project_c, lower_qb, lower_vb)
    x1 = x0 + product(attended1, lower_merge_full) + lower_mb

    b = layer_norm(x1, ln2_gain, ln2_shift)
    pre = product(b, expand_c) + expand_b
    hidden = low(gelu_parts(pre)[0])
    partial = low(product(hidden, shrink_c))
    x2 = x1 + (widen(partial) + widen(swap_cores(partial))) + shrink_b

    a2_own = layer_norm(x2, ln3_gain, ln3_shift)
    a2 = jnp.concatenate([a2_own, halo_rows(a2_own)], axis=0)
    packed2, logs2, attended2 = attention_forward(x2, a2, upper_project_c, upper_qb, upper_vb)

    def own_rows(values):
        return lax.dynamic_slice_in_dim(values, core * own, own, 0)

    x3 = own_rows(x2) + product(own_rows(attended2), upper_merge_full) + upper_mb
    normed = layer_norm(x3, ln4_gain, ln4_shift)
    rows_in = to_experts(normed)

    def gating(values):
        logits = product(values, router_w)
        raised = jnp.exp(logits - jnp.max(logits, axis=1, keepdims=True))
        return raised / jnp.sum(raised, axis=1, keepdims=True)

    mine = (jnp.arange(experts, dtype=jnp.int32) == here // copies).astype(WIDE)[None]
    probs_in = gating(rows_in)
    gate_in = jnp.sum(probs_in * mine, axis=1, keepdims=True)
    raw = product(grad_rows, shrink_e)
    before = product(rows_in, expand_e) + expert_expand_bias.astype(LOWTYPE).astype(WIDE)
    expert_hidden, slope = gelu_parts(before)
    expert_hidden = low(expert_hidden)
    once = (here % copies == 0).astype(WIDE)
    bias_here = product(low(mine), expert_bias) * once
    delta_gate = jnp.sum(widen(expert_hidden) * raw, axis=1, keepdims=True)
    delta_gate = delta_gate + jnp.sum(widen(grad_rows) * bias_here, axis=1, keepdims=True)
    dbefore = low(gate_in * raw * slope)
    dlogits = low(probs_in * delta_gate * (mine - gate_in))
    drows = over_features(dbefore, expand_e) + product(dlogits, router_t)
    returned_grad = to_patches(drows)
    returned = to_patches(over_features(expert_hidden, shrink_e))
    g_out = low(gate_in * widen(grad_rows))
    delta_expand_e = over_rows(rows_in, dbefore)
    delta_shrink_e = over_rows(g_out, expert_hidden)
    delta_expert_bias = jnp.sum(widen(dbefore), axis=0)
    delta_router = over_rows(rows_in, dlogits)
    delta_shrink_bias = (jnp.sum(widen(g_out), axis=0) * once)[:, None] * mine
    delta_expert_expand = expert_parts(delta_expand_e)
    delta_expert_shrink = expert_parts(delta_shrink_e).T

    probs = gating(normed)
    result = x3
    for k in range(2):
        gate = jnp.sum(widen(chosen[k]) * probs, axis=1, keepdims=True)
        picked = product(placed[k], returned) + product(chosen[k], expert_bias)
        result = result + gate * picked

    delta_normed = product(placed_any, returned_grad)
    dx3, dgain4, dshift4 = layer_norm_back(x3, ln4_gain, delta_normed)
    dx3 = output_grad + dx3
    dx3 = in_order(dx3, swap_cores(dx3), core, 0)
    half_lanes = (jnp.arange(width, dtype=jnp.int32) // share == core).astype(WIDE)

    def columns_of_half(values):
        return lax.dynamic_slice_in_dim(values, core * share, share, 1)

    def spread(vector):
        return lax.dynamic_update_slice_in_dim(jnp.zeros((width,), WIDE), vector, core * share, 0)

    def attention_backward(dresidual, residual, normed, packed, logs, attended, gain, project_c, merge):
        dmerged = low(dresidual)
        delta_merge_bias = jnp.sum(widen(dmerged), axis=0) * half_lanes
        delta_merge = over_rows(attended, columns_of_half(dmerged))
        merge_rows = lax.dynamic_slice_in_dim(merge, core * share, share, 0)
        dattended = low(over_features(dmerged, merge_rows))
        dpacked = attend_back(scalars, packed, dattended, logs, rows, halo, dim)
        dnormed = over_features(dpacked, project_c)
        far = swap_chips(low(dnormed[rows:]))
        delta_project = over_rows(normed, dpacked)
        bias_sums = jnp.sum(widen(dpacked), axis=0)
        mine_part = low(
            dnormed[:rows]
            + lax.dynamic_update_slice_in_dim(jnp.zeros((rows, width), WIDE), widen(far), mid_start, 0)
        )
        dnormed = widen(mine_part) + widen(swap_cores(mine_part))
        dinput, dgain, dshift = layer_norm_back(residual, gain, dnormed)
        sums = (
            dgain * half_lanes,
            dshift * half_lanes,
            spread(bias_sums[:share]),
            spread(bias_sums[2 * share :]),
            delta_merge_bias,
        )
        return dresidual + dinput, jnp.concatenate([delta_project, delta_merge], axis=1), sums

    dx2, upper_grads, upper_sums = attention_backward(
        dx3, x2, a2, packed2, logs2, attended2, ln3_gain, upper_project_c, upper_merge_full
    )
    third_mine, third_other = scatter_rows(upper_grads, core)

    dmlp = low(dx2)
    delta_shrink_b = jnp.sum(widen(dmlp), axis=0) * half_lanes
    delta_shrink = over_rows(hidden, dmlp)
    dpre = low(over_features(dmlp, shrink_c) * gelu_parts(pre)[1])
    shrink_mine, shrink_other = scatter_rows(delta_shrink, core)
    dnormed = low(over_features(dpre, expand_c))
    delta_expand = over_rows(b, dpre)
    delta_expand_b = jnp.sum(widen(dpre), axis=0)
    expand_mine, expand_other = scatter_rows(delta_expand, core)
    dinput, dgain2, dshift2 = layer_norm_back(x1, ln2_gain, widen(dnormed) + widen(swap_cores(dnormed)))
    dx1 = dx2 + dinput

    dx0, lower_grads, lower_sums = attention_backward(
        dx1, x0, a1, packed1, logs1, attended1, ln1_gain, lower_project_c, lower_merge_full
    )
    delta_patches = own_rows(dx0)

    sums = jnp.stack(
        list(lower_sums)
        + [dgain2 * half_lanes, dshift2 * half_lanes, delta_shrink_b]
        + list(upper_sums)
        + [dgain4, dshift4],
        axis=1,
    )
    expand_sums = delta_expand_b.reshape(devices, 1, hidden_part // 2) * (
        jnp.arange(2, dtype=jnp.int32)[None, :, None] == core
    ).astype(WIDE)
    small_grads = jnp.concatenate(
        [sums, expand_sums.reshape(width, extra), delta_router, delta_shrink_bias], axis=1
    )
    small_grads = jnp.pad(small_grads, ((0, 0), (0, 128 - small_grads.shape[1])))
    first_mine, first_other = scatter_rows(jnp.concatenate([lower_grads, small_grads], axis=1), core)

    def halves(mine_part, other_part):
        return jnp.stack(
            [
                jnp.where(core == 0, mine_part, other_part),
                jnp.where(core == 0, other_part, mine_part),
            ]
        )

    def attention_outputs(mine_part, other_part):
        both = widen(halves(mine_part, other_part))
        project = both[:, :, : 3 * share].reshape(2, part, 3, share).transpose(1, 2, 0, 3)
        merge = both[:, :, 3 * share : 4 * share].transpose(1, 0, 2)
        return project.reshape(part, 3 * width), merge.reshape(part, width)

    delta_lower_project, delta_lower_merge = attention_outputs(first_mine, first_other)
    delta_upper_project, delta_upper_merge = attention_outputs(third_mine, third_other)
    delta_lower_expand = (
        widen(halves(expand_mine, expand_other))
        .reshape(2, part, devices, hidden_part // 2)
        .transpose(1, 2, 0, 3)
        .reshape(part, -1)
    )
    delta_lower_shrink = widen(halves(shrink_mine, shrink_other)).reshape(hidden_part, width)
    vector_grads = widen(first_mine[:, 4 * share :]) + widen(first_other[:, 4 * share :])
    vector_t = vector_grads.T
    v = [vector_t[i] for i in range(count)]
    delta_lower_expand_bias = vector_grads[:, count : count + extra].reshape(hidden_part)
    delta_router_out = vector_grads[:, count + extra : count + extra + experts]
    delta_expert_shrink_bias = vector_t[count + extra + experts : count + extra + 2 * experts]
    return (
        result,
        delta_patches,
        v[0],
        v[1],
        delta_lower_project,
        v[2],
        v[3],
        delta_lower_merge,
        v[4],
        v[5],
        v[6],
        delta_lower_expand,
        delta_lower_expand_bias,
        delta_lower_shrink,
        v[7],
        v[8],
        v[9],
        delta_upper_project,
        v[10],
        v[11],
        delta_upper_merge,
        v[12],
        v[13],
        v[14],
        delta_router_out,
        delta_expert_expand,
        delta_expert_bias,
        delta_expert_shrink,
        delta_expert_shrink_bias,
    )


def solution(mesh):
    groups, parts = mesh.devices.shape
    inner = Mesh(mesh.devices.reshape(groups // 2, 2, parts // 2, 2), ALL)
    dp, seq = ("z", "y"), ("x", "c")
    rows, flat = P(ALL, None), P(ALL)
    in_specs = (
        (rows, P(dp, None), rows)
        + (flat, flat, rows, flat, flat, rows, flat)
        + (flat, flat, rows, flat, rows, flat)
        + (flat, flat, rows, flat, flat, rows, flat)
        + (flat, flat, rows, P(seq, dp), flat, P(dp, seq), P(None, ALL), rows)
    )
    out_specs = (
        (rows, rows)
        + (flat, flat, rows, flat, flat, rows, flat)
        + (flat, flat, rows, flat, rows, flat)
        + (flat, flat, rows, flat, flat, rows, flat)
        + (flat, flat, rows, P(seq, dp), flat, P(dp, seq), P(None, ALL))
    )
    return jax.shard_map(local, mesh=inner, in_specs=in_specs, out_specs=out_specs, check_vma=False)
```

```python
import functools
import math

import jax
import jax.numpy as jnp
from jax import lax
from jax.experimental import pallas as pl
from jax.experimental.pallas import tpu as pltpu
from jax.sharding import Mesh
from jax.sharding import PartitionSpec as P

HEADS = 12
CAP = 17
SLOTS = 24
LONG = 576
EDGE = 192
MASKED = -1000000000.0
EPSILON = 1e-06
LOWTYPE = jnp.bfloat16
WIDE = jnp.float32
ALL = ("z", "y", "x", "c")
CHIPS = ("z", "y", "x")
SWAP = [(0, 1), (1, 0)]


def dot(left, right, dims):
    return lax.dot_general(left, right, ((dims[0], dims[1]), ((), ())), preferred_element_type=WIDE)


def product(left, right):
    return dot(left, right, ((1,), (0,)))


def over_rows(left, right):
    return dot(left, right, ((0,), (0,)))


def over_features(left, right):
    return dot(left, right, ((1,), (1,)))


def low(values):
    return values.astype(LOWTYPE)


def widen(values):
    return values.astype(WIDE)


def swap_cores(values):
    return lax.ppermute(values, "c", SWAP)


def swap_chips(values):
    return lax.ppermute(values, "x", SWAP)


def in_order(mine, other, index, axis):
    first = jnp.where(index == 0, mine, other)
    second = jnp.where(index == 0, other, mine)
    return jnp.concatenate([first, second], axis=axis)


def norm_parts(values):
    center = values - jnp.mean(values, axis=-1, keepdims=True)
    spread = jnp.mean(center * center, axis=-1, keepdims=True)
    return center, lax.rsqrt(spread + EPSILON)


def layer_norm(values, gain, shift):
    center, scale = norm_parts(values)
    return low(center * scale * gain + shift)


def layer_norm_back(values, gain, grad):
    center, scale = norm_parts(values)
    hat = center * scale
    inner = grad * gain
    dvalues = scale * (
        inner
        - jnp.mean(inner, axis=-1, keepdims=True)
        - hat * jnp.mean(inner * hat, axis=-1, keepdims=True)
    )
    return dvalues, jnp.sum(grad * hat, axis=0), jnp.sum(grad, axis=0)


def gelu_parts(values):
    cdf = 0.5 + 0.5 * lax.erf(values * math.sqrt(0.5))
    pdf = jnp.exp(-0.5 * values * values) * (1.0 / math.sqrt(2.0 * math.pi))
    return values * cdf, cdf + values * pdf


def image_of(places, first_end, second_end):
    return (places >= first_end).astype(jnp.int32) + (places >= second_end).astype(jnp.int32)


def attention_places(scalars, rows, halo):
    x = scalars[0]
    edge_start = pl.multiple_of(x * (rows // 2), 64)
    mid_start = pl.multiple_of((1 - x) * (rows - halo), 64)
    mid_place = rows * x + mid_start
    halo_place = rows + x * ((rows - halo) - rows)
    return edge_start, mid_start, rows * x + edge_start, mid_place, halo_place


def edge_mask(place, count, first_end, second_end):
    row = image_of(place + lax.broadcasted_iota(jnp.int32, (count, 1), 0), first_end, second_end)
    column = image_of(place + lax.broadcasted_iota(jnp.int32, (1, count), 1), first_end, second_end)
    return (row == column) & (column != 1)


def mid_mask(mid_place, halo_place, count, first_end, second_end):
    row_places = mid_place + lax.broadcasted_iota(jnp.int32, (count, 1), 0)
    columns = lax.broadcasted_iota(jnp.int32, (1, 2 * count), 1)
    column_places = jnp.where(columns < count, mid_place + columns, halo_place + columns - count)
    row = image_of(row_places, first_end, second_end) == 1
    column = image_of(column_places, first_end, second_end) == 1
    return row & column, row


def lane_of_head(head, dim, lanes):
    lane = lax.broadcasted_iota(jnp.int32, (1, lanes), 1)
    return (lane >= head * dim) & (lane < (head + 1) * dim)


def only(values, lanes):
    return jnp.where(lanes, values, jnp.zeros_like(values))


def attend_kernel(scalars, packed, out, logs, *, rows, halo, dim):
    share = out.shape[1]
    first_end, second_end = scalars[1], scalars[2]
    edge_start, mid_start, edge_place, mid_place, halo_place = attention_places(scalars, rows, halo)
    half = rows // 2
    scale = 1.0 / math.sqrt(dim)
    mask_edge = edge_mask(edge_place, half, first_end, second_end)
    mask_mid, row_mid = mid_mask(mid_place, halo_place, halo, first_end, second_end)

    def one(queries, keys, values, mask):
        total, log_total = None, None
        for head in range(2):
            lanes = lane_of_head(head, dim, 128)
            scores = jnp.where(mask, over_features(only(queries, lanes), keys) * scale, MASKED)
            highest = jnp.max(scores, axis=-1, keepdims=True)
            raised = jnp.exp(scores - highest)
            sums = jnp.sum(raised, axis=-1, keepdims=True)
            weights = low(raised * (1.0 / sums))
            part = product(weights, only(values, lanes))
            total = part if total is None else total + part
            log_sum = highest + jnp.log(sums)
            log_total = log_sum if head == 0 else jnp.where(lanes, log_sum, log_total)
        return total, log_total

    def pair(index, carry):
        query_lanes = pl.ds(pl.multiple_of(index * 128, 128), 128)
        key_lanes = pl.ds(pl.multiple_of(share + index * 128, 128), 128)
        value_lanes = pl.ds(pl.multiple_of(2 * share + index * 128, 128), 128)
        edge = pl.ds(edge_start, half)
        mid = pl.ds(mid_start, halo)
        far = pl.ds(rows, halo)
        result, log_total = one(
            packed[edge, query_lanes], packed[edge, key_lanes], packed[edge, value_lanes], mask_edge
        )
        out[edge, query_lanes] = low(result)
        logs[edge, query_lanes] = log_total
        keys = jnp.concatenate([packed[mid, key_lanes], packed[far, key_lanes]], axis=0)
        values = jnp.concatenate([packed[mid, value_lanes], packed[far, value_lanes]], axis=0)
        result, log_total = one(packed[mid, query_lanes], keys, values, mask_mid)
        out[mid, query_lanes] = jnp.where(row_mid, low(result), out[mid, query_lanes])
        logs[mid, query_lanes] = jnp.where(row_mid, log_total, logs[mid, query_lanes])
        return carry

    lax.fori_loop(0, share // 128, pair, 0)


def attend_back_kernel(scalars, packed, grads, logs, out, *, rows, halo, dim):
    share = grads.shape[1]
    first_end, second_end = scalars[1], scalars[2]
    edge_start, mid_start, edge_place, mid_place, halo_place = attention_places(scalars, rows, halo)
    half = rows // 2
    scale = 1.0 / math.sqrt(dim)
    mask_edge = edge_mask(edge_place, half, first_end, second_end)
    mask_mid, _ = mid_mask(mid_place, halo_place, halo, first_end, second_end)

    def one(queries, keys, values, grad, log_total, mask):
        dquery, dkey, dvalue = None, None, None
        for head in range(2):
            lanes = lane_of_head(head, dim, 128)
            query, key, dout = only(queries, lanes), only(keys, lanes), only(grad, lanes)
            logs_here = log_total[:, head * dim : head * dim + 1]
            scores = jnp.where(mask, over_features(query, keys) * scale, MASKED)
            probs = jnp.exp(scores - logs_here)
            dprobs = over_features(dout, values)
            delta = jnp.sum(probs * dprobs, axis=-1, keepdims=True)
            dscores = low(probs * (dprobs - delta))
            parts = (
                product(dscores, key) * scale,
                over_rows(dscores, query) * scale,
                over_rows(low(probs), dout),
            )
            if head == 0:
                dquery, dkey, dvalue = parts
            else:
                dquery, dkey, dvalue = dquery + parts[0], dkey + parts[1], dvalue + parts[2]
        return low(dquery), low(dkey), low(dvalue)

    out[...] = jnp.zeros_like(out)

    def pair(index, carry):
        query_lanes = pl.ds(pl.multiple_of(index * 128, 128), 128)
        key_lanes = pl.ds(pl.multiple_of(share + index * 128, 128), 128)
        value_lanes = pl.ds(pl.multiple_of(2 * share + index * 128, 128), 128)
        edge = pl.ds(edge_start, half)
        mid = pl.ds(mid_start, halo)
        far = pl.ds(rows, halo)
        dquery, dkey, dvalue = one(
            packed[edge, query_lanes],
            packed[edge, key_lanes],
            packed[edge, value_lanes],
            grads[edge, query_lanes],
            logs[edge, query_lanes],
            mask_edge,
        )
        out[edge, query_lanes] = dquery
        out[edge, key_lanes] = dkey
        out[edge, value_lanes] = dvalue
        keys = jnp.concatenate([packed[mid, key_lanes], packed[far, key_lanes]], axis=0)
        values = jnp.concatenate([packed[mid, value_lanes], packed[far, value_lanes]], axis=0)
        dquery, dkey, dvalue = one(
            packed[mid, query_lanes],
            keys,
            values,
            grads[mid, query_lanes],
            logs[mid, query_lanes],
            mask_mid,
        )
        out[mid, query_lanes] = out[mid, query_lanes] + dquery
        out[mid, key_lanes] = out[mid, key_lanes] + dkey[:halo]
        out[mid, value_lanes] = out[mid, value_lanes] + dvalue[:halo]
        out[far, key_lanes] = dkey[halo:]
        out[far, value_lanes] = dvalue[halo:]
        return carry

    lax.fori_loop(0, share // 128, pair, 0)


def kernel_call(body, outs, operands, flops):
    return pl.pallas_call(
        body,
        out_shape=outs,
        in_specs=[pl.BlockSpec(memory_space=pltpu.SMEM)]
        + [pl.BlockSpec(memory_space=pltpu.VMEM)] * (len(operands) - 1),
        out_specs=[pl.BlockSpec(memory_space=pltpu.VMEM)] * len(outs),
        compiler_params=pltpu.CompilerParams(vmem_limit_bytes=48 * 1024 * 1024),
        cost_estimate=pl.CostEstimate(flops=flops, bytes_accessed=8_000_000, transcendentals=1_700_000),
    )(*operands)


def attend(scalars, packed, rows, halo, dim):
    share = packed.shape[1] // 3
    return kernel_call(
        functools.partial(attend_kernel, rows=rows, halo=halo, dim=dim),
        [jax.ShapeDtypeStruct((rows, share), LOWTYPE), jax.ShapeDtypeStruct((rows, share), WIDE)],
        [scalars, packed],
        1_700_000_000,
    )


def attend_back(scalars, packed, grads, logs, rows, halo, dim):
    [out] = kernel_call(
        functools.partial(attend_back_kernel, rows=rows, halo=halo, dim=dim),
        [jax.ShapeDtypeStruct(packed.shape, LOWTYPE)],
        [scalars, packed, grads, logs],
        4_000_000_000,
    )
    return out


def attention_grads_kernel(normed, dpacked, attended, dmerged, *refs):
    out, width = refs[-1], dmerged.shape[1]
    for i in range(3):
        part = over_rows(normed[...], dpacked[:, i * width : (i + 1) * width])
        out[:, i * width : (i + 1) * width] = low(part)
    out[:, 3 * width : 4 * width] = low(over_rows(attended[...], dmerged[...]))
    if len(refs) == 2:
        out[:, 4 * width :] = low(refs[0][...])


def attention_grads(*operands):
    normed, dpacked, _, dmerged = operands[:4]
    lanes = dpacked.shape[1] + dmerged.shape[1] + sum(o.shape[1] for o in operands[4:])
    inside = pl.BlockSpec(memory_space=pltpu.VMEM)
    return pl.pallas_call(
        attention_grads_kernel,
        out_shape=jax.ShapeDtypeStruct((normed.shape[1], lanes), LOWTYPE),
        in_specs=[inside] * len(operands),
        out_specs=inside,
        compiler_params=pltpu.CompilerParams(vmem_limit_bytes=40 * 1024 * 1024),
        cost_estimate=pl.CostEstimate(
            flops=2 * normed.shape[0] * normed.shape[1] * lanes,
            bytes_accessed=8_000_000,
            transcendentals=0,
        ),
    )(*operands)


def pick(block, index):
    return lax.dynamic_index_in_dim(block, index, 0, keepdims=False)


def xor_pairs(size, flip):
    return [(i, i ^ flip) for i in range(size)]


def assemble_kernel(coords, *refs, parts):
    blocks, outs = refs[: len(refs) - len(parts)], refs[len(refs) - len(parts) :]
    count = blocks[0].shape[0]
    for k, block in enumerate(blocks):
        chip = (coords[0] ^ (k >> 2)) * 4 + (coords[1] ^ ((k >> 1) & 1)) * 2 + (coords[2] ^ (k & 1))
        start = 0
        for out, (width, groups) in zip(outs, parts):
            for group in range(groups):
                place = pl.multiple_of((chip * groups + group) * count, 16)
                out[pl.ds(place, count), :] = block[:, start : start + width]
                start += width


def assemble(coords, blocks, parts):
    count, width = blocks[0].shape
    inside = pl.BlockSpec(memory_space=pltpu.VMEM)
    return pl.pallas_call(
        functools.partial(assemble_kernel, parts=parts),
        out_shape=[
            jax.ShapeDtypeStruct((len(blocks) * count * groups, lanes), LOWTYPE)
            for lanes, groups in parts
        ],
        in_specs=[pl.BlockSpec(memory_space=pltpu.SMEM)] + [inside] * len(blocks),
        out_specs=[inside] * len(parts),
        compiler_params=pltpu.CompilerParams(vmem_limit_bytes=40 * 1024 * 1024),
        cost_estimate=pl.CostEstimate(
            flops=0, bytes_accessed=4 * len(blocks) * count * width, transcendentals=0
        ),
    )(coords, *blocks)


def tie(*values):
    return lax.optimization_barrier(values)


def gather_z(pair, after=()):
    if lax.axis_size("z") != 4:
        return [lax.all_gather(pair, CHIPS, axis=0, tiled=True), pair]
    if after:
        pair, after = tie(pair, after)
    return [pair] + [lax.ppermute(pair, "z", xor_pairs(4, k)) for k in (1, 2, 3)]


def gather_plane(along):
    if lax.axis_size("z") != 4:
        return []
    return [(swap_chips(here), lax.ppermute(here, "y", SWAP)) for here in along]


def gather_end(along, plane, parts, x_first):
    if lax.axis_size("z") != 4:
        whole, count = along[0], along[1].shape[0]
        outs, start = [], 0
        for lanes, groups in parts:
            piece = whole[:, start : start + lanes * groups]
            piece = piece.reshape(-1, count, groups, lanes).transpose(0, 2, 1, 3)
            outs.append(piece.reshape(-1, lanes))
            start += lanes * groups
        return outs, ()
    blocks, across = [], []
    for k, (here, (by_x, by_y)) in enumerate(zip(along, plane)):
        if k in x_first:
            blocks += [here, by_x, by_y, lax.ppermute(by_x, "y", SWAP)]
            across += [by_x]
        else:
            blocks += [here, by_x, by_y, swap_chips(by_y)]
            across += [by_x, blocks[-1]]
    coords = jnp.stack([lax.axis_index(name) for name in CHIPS]).astype(jnp.int32)
    return assemble(coords, blocks, parts), tuple(across)


def added(left, right):
    return low(widen(left) + widen(right))


def at(values, index, axis):
    return lax.dynamic_index_in_dim(values, index, axis, keepdims=False)


def pairs_first(grads):
    if lax.axis_size("z") != 4:
        return lax.psum_scatter(low(grads), CHIPS, scatter_dimension=0, tiled=True)
    z, y, x = [lax.axis_index(name) for name in CHIPS]
    view = low(grads).reshape(2, 2, 2, 2, grads.shape[0] // 16, grads.shape[1])
    near, far = at(view, z // 2, 0), at(view, 1 - z // 2, 0)
    from_y, from_x = lax.ppermute(at(near, 1 - y, 1), "y", SWAP), swap_chips(at(far, 1 - x, 2))
    return at(near, y, 1), from_y, at(far, x, 2), from_x


def pairs_second(state):
    if lax.axis_size("z") != 4:
        return state
    y, x = lax.axis_index("y"), lax.axis_index("x")
    near, far = added(*state[:2]), added(*state[2:])
    from_x, from_y = swap_chips(at(near, 1 - x, 1)), lax.ppermute(at(far, 1 - y, 1), "y", SWAP)
    return at(near, x, 1), from_x, at(far, y, 1), from_y


def pairs_z(state):
    if lax.axis_size("z") != 4:
        return state
    low_bit = lax.axis_index("z") % 2
    near, far = added(*state[:2]), added(*state[2:])
    sent = (at(near, 1 - low_bit, 0), at(far, low_bit, 0), at(far, 1 - low_bit, 0))
    got = [lax.ppermute(piece, "z", xor_pairs(4, k + 1)) for k, piece in enumerate(sent)]
    return [at(near, low_bit, 0)] + got


def summed_everywhere(values):
    if lax.axis_size("z") != 4:
        return lax.psum(values, ALL)
    for name, pairs in (("c", SWAP), ("x", SWAP), ("y", SWAP), ("z", xor_pairs(4, 1)), ("z", xor_pairs(4, 2))):
        values = values + lax.ppermute(values, name, pairs)
    return values


def scatter_y(grads):
    if lax.axis_size("z") != 4:
        return lax.psum_scatter(low(grads), CHIPS, scatter_dimension=0, tiled=True)
    y = lax.axis_index("y")
    view = low(grads).reshape(4, 2, 2, grads.shape[0] // 16, grads.shape[1])
    return at(view, y, 1), lax.ppermute(at(view, 1 - y, 1), "y", SWAP)


def scatter_x(state):
    if lax.axis_size("z") != 4:
        return state
    x, values = lax.axis_index("x"), added(*state)
    return at(values, x, 1), swap_chips(at(values, 1 - x, 1))


def scatter_z(state):
    if lax.axis_size("z") != 4:
        return state
    z, values = lax.axis_index("z"), added(*state)
    sent = [lax.ppermute(at(values, z ^ k, 0), "z", xor_pairs(4, k)) for k in (1, 2, 3)]
    return [at(values, z, 0)] + sent


def scatter_end(state):
    if lax.axis_size("z") != 4:
        return widen(state)
    return widen(state[0]) + widen(state[1]) + widen(state[2]) + widen(state[3])


def exchange_halves(first, second, core):
    mine = jnp.where(core == 0, first, second)
    other = widen(swap_cores(low(jnp.where(core == 0, second, first))))
    return mine, other


def cut_kernel(place, weight, *outs):
    for k, out in enumerate(outs):

        @pl.when(pl.program_id(0) == k)
        def _(out=out):
            out[...] = low(weight[...])


def cut_columns(weight, place):
    rows, units = weight.shape[0], weight.shape[1] // 4
    return pl.pallas_call(
        cut_kernel,
        grid_spec=pltpu.PrefetchScalarGridSpec(
            num_scalar_prefetch=1,
            grid=(4,),
            in_specs=[pl.BlockSpec((rows, units), lambda i, p: (0, p[0] ^ i))],
            out_specs=[pl.BlockSpec((rows, units), lambda i, p: (0, 0))] * 4,
        ),
        out_shape=[jax.ShapeDtypeStruct((rows, units), LOWTYPE)] * 4,
        compiler_params=pltpu.CompilerParams(vmem_limit_bytes=32 * 1024 * 1024),
        cost_estimate=pl.CostEstimate(flops=0, bytes_accessed=6 * weight.size, transcendentals=0),
    )(place, weight)


def stack_kernel(place, *refs):
    blocks, out = refs[:4], refs[4]
    count = blocks[0].shape[0]
    for k, block in enumerate(blocks):
        out[pl.ds(pl.multiple_of((place[0] ^ k) * count, 16), count), :] = block[...]


def stack_rows(place, blocks):
    count, width = blocks[0].shape
    inside = pl.BlockSpec(memory_space=pltpu.VMEM)
    return pl.pallas_call(
        stack_kernel,
        out_shape=jax.ShapeDtypeStruct((4 * count, width), LOWTYPE),
        in_specs=[pl.BlockSpec(memory_space=pltpu.SMEM)] + [inside] * 4,
        out_specs=inside,
        compiler_params=pltpu.CompilerParams(vmem_limit_bytes=32 * 1024 * 1024),
        cost_estimate=pl.CostEstimate(flops=0, bytes_accessed=16 * count * width, transcendentals=0),
    )(place, *blocks)


def join_kernel(place, *refs):
    for k in range(4):

        @pl.when(pl.program_id(0) == k)
        def _(k=k):
            refs[4][...] = widen(refs[k][...])


def join_columns(place, pieces):
    rows, units = pieces[0].shape
    return pl.pallas_call(
        join_kernel,
        grid_spec=pltpu.PrefetchScalarGridSpec(
            num_scalar_prefetch=1,
            grid=(4,),
            in_specs=[pl.BlockSpec((rows, units), lambda i, p: (0, 0))] * 4,
            out_specs=pl.BlockSpec((rows, units), lambda i, p: (0, p[0] ^ i)),
        ),
        out_shape=jax.ShapeDtypeStruct((rows, 4 * units), WIDE),
        compiler_params=pltpu.CompilerParams(vmem_limit_bytes=40 * 1024 * 1024),
        cost_estimate=pl.CostEstimate(flops=0, bytes_accessed=24 * rows * units, transcendentals=0),
    )(place, *pieces)


def column_sums(values):
    return product(jnp.ones((8, values.shape[0]), LOWTYPE), values)[0]


def halves_of(weight, width):
    parts = [weight[:, i : i + width] for i in range(0, weight.shape[1], width)]
    return tuple(
        jnp.concatenate([p[:, h * width // 2 : (h + 1) * width // 2] for p in parts], axis=1)
        for h in range(2)
    )


def cut_dense(project, merge, small, expand, shrink, upper_project, upper_merge):
    width = merge.shape[1]
    half_rows = shrink.shape[0] // 2
    project, merge = halves_of(project, width), halves_of(merge, width)
    upper_project, upper_merge = halves_of(upper_project, width), halves_of(upper_merge, width)
    expand, shrink = halves_of(expand, expand.shape[1]), halves_of(shrink, width)
    return [
        (
            jnp.concatenate([project[h], merge[h], small], axis=1),
            jnp.concatenate([expand[h], upper_project[h], upper_merge[h]], axis=1),
            jnp.concatenate([shrink[h][:half_rows], shrink[h][half_rows:]], axis=1),
        )
        for h in range(2)
    ]


def prologue_kernel(core, *refs, count):
    operands = count + 9
    sources, outs = refs[:operands], refs[operands : operands + 6]
    table, small, sems = refs[operands + 6 : operands + 9]
    inside = refs[operands + 9 :]
    copies = [
        pltpu.make_async_copy(source, target, sems.at[i])
        for i, (source, target) in enumerate(zip(sources, inside))
    ]
    for copy in copies:
        copy.start()
    for copy in copies:
        copy.wait()
    vectors, (expand_bias, router, bias), weights = inside[:count], inside[count : count + 3], inside[count + 3 :]
    part = router.shape[0]
    table[...] = jnp.zeros_like(table)
    for i, vector in enumerate(vectors):
        table[i : i + 1, 0:part] = vector[...].reshape(1, part)
    biases = expand_bias[...].reshape(1, 4 * part)
    for q in range(4):
        table[16 + q : 17 + q, 0:part] = biases[:, q * part : (q + 1) * part]
    small[...] = table[...].T
    small[0:part, 32 : 32 + router.shape[1]] = router[...]
    small[0:part, 64 : 64 + bias.shape[1]] = bias[...]
    values = [ref[...] for ref in weights]
    cut = cut_dense(values[0], values[1], small[0:part, :], *values[2:])
    first = core[0] == 0
    for i in range(3):
        outs[i][...] = low(jnp.where(first, cut[0][i], cut[1][i]))
        outs[3 + i][...] = low(jnp.where(first, cut[1][i], cut[0][i]))


def prologue(core, vectors, expand_bias, router, bias, weights):
    part = router.shape[0]
    if lax.axis_size("z") != 4:
        rows = [jnp.stack(vectors), jnp.zeros((16 - len(vectors), part), WIDE)]
        rows += [expand_bias.reshape(4, part), jnp.zeros((12, part), WIDE)]
        small = jnp.concatenate([jnp.concatenate(rows).T, router, bias], axis=1)
        small = jnp.pad(small, ((0, 0), (0, 128 - small.shape[1])))
        cut = cut_dense(weights[0], weights[1], small, *weights[2:])
        picked = [[jnp.where(core == h, a, b) for a, b in zip(*cut)] for h in range(2)]
        return [low(v) for v in picked[0]], [low(v) for v in picked[1]]
    lanes = [weights[0].shape[1] // 2 + weights[1].shape[1] // 2 + 128]
    lanes += [sum(w.shape[1] // 2 for w in (weights[2], weights[4], weights[5]))]
    shapes = [(part, lanes[0]), (part, lanes[1]), (weights[3].shape[0] // 2, weights[3].shape[1])]
    inside = pl.BlockSpec(memory_space=pltpu.VMEM)
    operands = [*vectors, expand_bias, router, bias, *weights]
    outs = pl.pallas_call(
        functools.partial(prologue_kernel, count=len(vectors)),
        out_shape=[jax.ShapeDtypeStruct(shape, LOWTYPE) for shape in shapes * 2],
        in_specs=[pl.BlockSpec(memory_space=pltpu.SMEM)]
        + [pl.BlockSpec(memory_space=pl.ANY)] * len(operands),
        out_specs=[inside] * 6,
        scratch_shapes=[
            pltpu.VMEM((128, 128), WIDE),
            pltpu.VMEM((128, 128), WIDE),
            pltpu.SemaphoreType.DMA((len(operands),)),
        ]
        + [pltpu.VMEM(operand.shape, WIDE) for operand in operands],
        compiler_params=pltpu.CompilerParams(vmem_limit_bytes=60 * 1024 * 1024),
        cost_estimate=pl.CostEstimate(flops=0, bytes_accessed=2_500_000, transcendentals=0),
    )(core.reshape(1).astype(jnp.int32), *operands)
    return outs[:3], outs[3:]


def local(
    patches,
    image_lengths,
    expert_ids,
    lower_norm_gain,
    lower_norm_shift,
    lower_project,
    lower_query_bias,
    lower_value_bias,
    lower_merge,
    lower_merge_bias,
    lower_second_gain,
    lower_second_shift,
    lower_expand,
    lower_expand_bias,
    lower_shrink,
    lower_shrink_bias,
    upper_norm_gain,
    upper_norm_shift,
    upper_project,
    upper_query_bias,
    upper_value_bias,
    upper_merge,
    upper_merge_bias,
    upper_second_gain,
    upper_second_shift,
    router,
    expert_expand,
    expert_expand_bias,
    expert_shrink,
    expert_shrink_bias,
    output_grad,
):
    x, core = lax.axis_index("x"), lax.axis_index("c")
    devices = lax.axis_size(ALL)
    here = lax.axis_index(ALL)
    own, width = patches.shape
    rows = 2 * own
    dim = width // HEADS
    halo = rows - EDGE
    share = width // 2
    experts = router.shape[1]
    copies = devices // experts
    slots = experts * SLOTS
    part = lower_norm_gain.shape[0]
    lengths = image_lengths[0]
    scalars = jnp.stack([x, lengths[0], lengths[0] + lengths[1]]).astype(jnp.int32)
    mid_start = (1 - x) * (rows - halo)

    def halo_rows(full):
        count = halo // 2
        piece = lax.dynamic_slice_in_dim(full, mid_start + core * count, count, 0)
        got = swap_chips(piece)
        return in_order(got, swap_cores(got), core, 0)

    vectors = [
        lower_norm_gain,
        lower_norm_shift,
        lower_query_bias,
        lower_value_bias,
        lower_merge_bias,
        lower_second_gain,
        lower_second_shift,
        lower_shrink_bias,
        upper_norm_gain,
        upper_norm_shift,
        upper_query_bias,
        upper_value_bias,
        upper_merge_bias,
        upper_second_gain,
        upper_second_shift,
    ]
    count = len(vectors)
    shares, others = prologue(
        core,
        vectors,
        lower_expand_bias,
        router,
        expert_shrink_bias.T,
        [lower_project, lower_merge, lower_expand, lower_shrink, upper_project, upper_merge],
    )
    got = [swap_cores(other) for other in others]
    pair_1 = in_order(shares[0], got[0], core, 0)
    hidden_half = lower_expand.shape[1] // 2
    pair_2 = in_order(shares[1], got[1], core, 0)
    pair_3 = pair_2[:, hidden_half:]
    pair_2 = jnp.concatenate(
        [pair_2[:, :hidden_half], in_order(shares[2], got[2], core, 1)], axis=1
    )
    along_1 = gather_z(pair_1)
    (lower_project_c, lower_merge_c, table), _ = gather_end(
        along_1, gather_plane(along_1), ((3 * share, 1), (share, 1), (128, 1)), (0, 2)
    )
    seat = (2 * x + core).reshape(1).astype(jnp.int32)
    expand_cut, shrink_cut = cut_columns(expert_expand, seat), cut_columns(expert_shrink.T, seat)
    table, expand_cut, shrink_cut = lax.optimization_barrier((table, expand_cut, shrink_cut))
    along_2 = gather_z(pair_2, tuple(along_1[1:2]))
    (expand_c, shrink_half), crossed = gather_end(
        along_2, gather_plane(along_2), ((hidden_half, 1), (share, 4)), (0, 2)
    )
    upper_c = lax.all_gather(pair_3, CHIPS, axis=0, tiled=True)
    upper_project_c, upper_merge_c = upper_c[:, : 3 * share], upper_c[:, 3 * share :]
    lower_merge_full = in_order(lower_merge_c, swap_cores(lower_merge_c), core, 1)
    shrink_parts = shrink_half.reshape(2, hidden_half, share)
    shrink_c = in_order(pick(shrink_parts, core), swap_cores(pick(shrink_parts, 1 - core)), core, 1)
    table_t = table.T
    wide_t = widen(table_t[:32])
    (
        ln1_gain,
        ln1_shift,
        lower_qb,
        lower_vb,
        lower_mb,
        ln2_gain,
        ln2_shift,
        shrink_b,
        ln3_gain,
        ln3_shift,
        upper_qb,
        upper_vb,
        upper_mb,
        ln4_gain,
        ln4_shift,
    ) = [wide_t[i] for i in range(count)]
    expand_b = wide_t[16:20].reshape(4, devices, part).transpose(1, 0, 2).reshape(2, hidden_half)
    expand_b = pick(expand_b, core)
    router_w = table[:, 32 : 32 + experts]
    router_t = table_t[32 : 32 + experts]
    expert_bias = table_t[64 : 64 + experts]

    def between(values, k):
        return lax.ppermute(values, ("x", "c"), xor_pairs(4, k))

    def whole_expert(pieces):
        if crossed:
            pieces, _ = lax.optimization_barrier((pieces, crossed))
        across = between(pieces[2], 2)
        last, _ = tie(pieces[3], across)
        return [pieces[0], between(pieces[1], 1), across, between(last, 3)]

    def expert_parts(grads):
        count = grads.shape[0] // 4
        pieces = [
            lax.dynamic_slice_in_dim(grads, (seat[0] ^ k) * count, count, 0) for k in range(4)
        ]
        far_piece = between(pieces[2], 2)
        last, _ = tie(pieces[3], far_piece)
        return [pieces[0], between(pieces[1], 1), far_piece, between(last, 3)]

    expand_e = whole_expert(expand_cut)
    shrink_e = whole_expert(shrink_cut)

    order = lax.broadcasted_iota(jnp.int32, (own, own), 0)
    before_it = low(order > lax.broadcasted_iota(jnp.int32, (own, own), 1))
    chosen = [
        low(expert_ids[:, k : k + 1] == jnp.arange(experts, dtype=jnp.int32)[None]) for k in range(2)
    ]
    earlier = product(before_it, chosen[0] + chosen[1])
    places = [
        expert_ids[:, k] * SLOTS
        + jnp.sum(widen(chosen[k]) * earlier, axis=1).astype(jnp.int32)
        for k in range(2)
    ]
    placed = [
        low(place[:, None] == jnp.arange(slots, dtype=jnp.int32)[None]) for place in places
    ]
    placed_any = placed[0] + placed[1]

    def to_experts(values):
        sent = low(over_rows(placed_any, values)).reshape(experts, SLOTS, width)
        if copies > 1:
            sent = jnp.repeat(sent, copies, axis=0)
        got = lax.all_to_all(sent, ALL, 0, 0, tiled=True)
        return got.reshape(devices * SLOTS, width)

    def to_patches(values):
        got = lax.all_to_all(low(values).reshape(devices, SLOTS, width), ALL, 0, 0, tiled=True)
        if copies > 1:
            got = low(jnp.sum(widen(got.reshape(experts, copies, SLOTS, width)), axis=1))
        return got.reshape(slots, width)

    grads_sent = low(output_grad)

    full = in_order(patches, swap_cores(patches), core, 0)
    x0 = widen(full)

    def half(vector):
        return lax.dynamic_slice_in_dim(vector, core * share, share, 0)

    def attention_forward(residual, normed, project_c, query_bias, value_bias):
        bias = jnp.concatenate([half(query_bias), jnp.zeros((share,), WIDE), half(value_bias)])
        packed = low(product(normed, project_c) + bias)
        attended, logs = attend(scalars, packed, rows, halo, dim)
        attended_full = in_order(attended, swap_cores(attended), core, 1)
        return packed, logs, attended_full

    a1 = layer_norm(jnp.concatenate([x0, widen(halo_rows(full))], axis=0), ln1_gain, ln1_shift)
    packed1, logs1, attended1 = attention_forward(x0, a1, lower_project_c, lower_qb, lower_vb)
    x1 = x0 + product(attended1, lower_merge_full) + lower_mb

    b = layer_norm(x1, ln2_gain, ln2_shift)
    pre = product(b, expand_c) + expand_b
    hidden = low(gelu_parts(pre)[0])
    upper_merge_full = in_order(upper_merge_c, swap_cores(upper_merge_c), core, 1)
    hidden_full = in_order(hidden, swap_cores(hidden), core, 1)
    partial = low(product(hidden, shrink_c))
    x2 = x1 + (widen(partial) + widen(swap_cores(partial))) + shrink_b

    a2_own = layer_norm(x2, ln3_gain, ln3_shift)
    a2 = jnp.concatenate([a2_own, halo_rows(a2_own)], axis=0)
    a2, expand_e[2] = tie(a2, expand_e[2])
    packed2, logs2, attended2 = attention_forward(x2, a2, upper_project_c, upper_qb, upper_vb)

    attended2, expand_e[3], grad_rows = tie(attended2, expand_e[3], to_experts(grads_sent))

    def own_rows(values):
        return lax.dynamic_slice_in_dim(values, core * own, own, 0)

    x3 = own_rows(x2) + product(own_rows(attended2), upper_merge_full) + upper_mb
    normed = layer_norm(x3, ln4_gain, ln4_shift)
    rows_in = to_experts(normed)
    rows_in, expand_e, shrink_e[2] = tie(rows_in, expand_e, shrink_e[2])
    expand_e, shrink_e = stack_rows(seat, expand_e), stack_rows(seat, shrink_e)

    def gating(values):
        logits = product(values, router_w)
        raised = jnp.exp(logits - jnp.max(logits, axis=1, keepdims=True))
        return raised / jnp.sum(raised, axis=1, keepdims=True)

    mine = (jnp.arange(experts, dtype=jnp.int32) == here // copies).astype(WIDE)[None]
    probs_in = gating(rows_in)
    gate_in = jnp.sum(probs_in * mine, axis=1, keepdims=True)
    raw = product(grad_rows, shrink_e)
    before = product(rows_in, expand_e) + expert_expand_bias.astype(LOWTYPE).astype(WIDE)
    expert_hidden, slope = gelu_parts(before)
    expert_hidden = low(expert_hidden)
    once = (here % copies == 0).astype(WIDE)
    bias_here = product(low(mine), expert_bias) * once
    delta_gate = jnp.sum(widen(expert_hidden) * raw, axis=1, keepdims=True)
    delta_gate = delta_gate + jnp.sum(widen(grad_rows) * bias_here, axis=1, keepdims=True)
    dbefore = low(gate_in * raw * slope)
    dlogits = low(probs_in * delta_gate * (mine - gate_in))
    drows = over_features(dbefore, expand_e) + product(dlogits, router_t)
    returned_grad = to_patches(drows)
    returned = to_patches(over_features(expert_hidden, shrink_e))
    g_out = low(gate_in * widen(grad_rows))
    delta_expand_e = over_rows(rows_in, dbefore)
    delta_shrink_e = over_rows(g_out, expert_hidden)
    delta_expert_bias = column_sums(dbefore)
    delta_router = over_rows(rows_in, dlogits)
    delta_shrink_e = low(delta_shrink_e)
    expand_pieces = expert_parts(low(delta_expand_e))
    returned_grad, expand_pieces[1], expand_pieces[2], delta_shrink_e = tie(
        returned_grad, expand_pieces[1], expand_pieces[2], delta_shrink_e
    )
    delta_shrink_bias = (column_sums(g_out) * once)[:, None] * mine

    delta_normed = product(placed_any, returned_grad)
    dx3, dgain4, dshift4 = layer_norm_back(x3, ln4_gain, delta_normed)
    dx3 = output_grad + dx3
    dx3 = in_order(dx3, swap_cores(dx3), core, 0)
    half_lanes = (jnp.arange(width, dtype=jnp.int32) // share == core).astype(WIDE)

    def columns_of_half(values):
        return lax.dynamic_slice_in_dim(values, core * share, share, 1)

    def spread(vector):
        return lax.dynamic_update_slice_in_dim(jnp.zeros((width,), WIDE), vector, core * share, 0)

    def attention_backward(
        dresidual, residual, normed, packed, logs, attended, gain, project_c, merge, waiting
    ):
        dmerged = low(dresidual)
        delta_merge_bias = column_sums(dmerged) * half_lanes
        merge_rows = lax.dynamic_slice_in_dim(merge, core * share, share, 0)
        dattended = low(over_features(dmerged, merge_rows))
        dpacked = attend_back(scalars, packed, dattended, logs, rows, halo, dim)
        dnormed = over_features(dpacked, project_c)
        dnormed, waiting = tie(dnormed, waiting)
        far = swap_chips(low(dnormed[rows:]))
        bias_sums = column_sums(dpacked)
        mine_part = low(
            dnormed[:rows]
            + lax.dynamic_update_slice_in_dim(jnp.zeros((rows, width), WIDE), widen(far), mid_start, 0)
        )
        dnormed = widen(mine_part) + widen(swap_cores(mine_part))
        dinput, dgain, dshift = layer_norm_back(residual, gain, dnormed)
        sums = (
            dgain * half_lanes,
            dshift * half_lanes,
            spread(bias_sums[:share]),
            spread(bias_sums[2 * share :]),
            delta_merge_bias,
        )
        outs = dresidual + dinput, (normed, dpacked, attended, columns_of_half(dmerged)), sums, far
        return *outs, waiting

    dx2, upper_grads, upper_sums, far, expand_pieces[3] = attention_backward(
        dx3,
        x2,
        a2,
        packed2,
        logs2,
        attended2,
        ln3_gain,
        upper_project_c,
        upper_merge_full,
        expand_pieces[3],
    )
    delta_shrink_e, _ = tie(delta_shrink_e, far)
    shrink_pieces = expert_parts(delta_shrink_e)
    third = scatter_y(attention_grads(*upper_grads))

    dmlp = low(dx2)
    delta_shrink_b = column_sums(dmlp) * half_lanes
    delta_shrink = low(over_rows(hidden_full, columns_of_half(dmlp)))
    delta_shrink = delta_shrink.reshape(-1, 4, 2 * part, share).transpose(0, 2, 1, 3)
    dpre = low(over_features(dmlp, shrink_c) * gelu_parts(pre)[1])
    dpre, shrink_pieces[2] = tie(dpre, shrink_pieces[2])
    dnormed = low(over_features(dpre, expand_c))
    delta_expand = low(over_rows(b, dpre))
    delta_expand_b = column_sums(dpre)
    second = pairs_first(
        jnp.concatenate([delta_expand, delta_shrink.reshape(width, 4 * share)], axis=1)
    )
    dinput, dgain2, dshift2 = layer_norm_back(x1, ln2_gain, widen(dnormed) + widen(swap_cores(dnormed)))
    dx1 = dx2 + dinput
    dx1, third, returned, shrink_pieces[3] = tie(dx1, third, returned, shrink_pieces[3])
    third = scatter_x(third)

    dx0, lower_grads, lower_sums, _, (third, second) = attention_backward(
        dx1,
        x0,
        a1,
        packed1,
        logs1,
        attended1,
        ln1_gain,
        lower_project_c,
        lower_merge_full,
        (third, second),
    )
    second = pairs_second(second)
    third = scatter_z(third)
    dx0, returned = tie(dx0, returned)
    probs = gating(normed)
    result = x3
    for k in range(2):
        gate = jnp.sum(widen(chosen[k]) * probs, axis=1, keepdims=True)
        picked = product(placed[k], returned) + product(chosen[k], expert_bias)
        result = result + gate * picked

    delta_patches = own_rows(dx0)

    expand_sums = lax.dynamic_update_slice_in_dim(
        jnp.zeros((2 * hidden_half,), WIDE), delta_expand_b, core * hidden_half, 0
    )
    expand_sums = expand_sums.reshape(devices, 4, part).transpose(1, 0, 2).reshape(4, width)
    sums = jnp.concatenate(
        [
            jnp.stack(
                [jnp.zeros((width,), WIDE)] * 2
                + list(lower_sums[2:])
                + [dgain2 * half_lanes, dshift2 * half_lanes, delta_shrink_b]
                + list(upper_sums)
                + [dgain4, dshift4, jnp.zeros((width,), WIDE)]
            ),
            expand_sums,
            jnp.zeros((12, width), WIDE),
        ]
    )
    small_grads = jnp.concatenate([sums.T, delta_router, delta_shrink_bias], axis=1)
    small_grads = jnp.pad(small_grads, ((0, 0), (0, 128 - small_grads.shape[1])))
    first = pairs_first(attention_grads(*lower_grads, small_grads))
    first, third, expand_pieces, shrink_pieces = tie(first, third, expand_pieces, shrink_pieces)
    third = scatter_end(third)
    delta_expert_expand = join_columns(seat, expand_pieces)
    delta_expert_shrink = join_columns(seat, shrink_pieces)
    norm_sums = jnp.concatenate([jnp.stack(lower_sums[:2]), jnp.zeros((6, width), WIDE)])
    first, second, norm_sums, delta_expert_expand = tie(
        pairs_second(first), second, norm_sums, delta_expert_expand
    )
    first, second, norm_sums = pairs_z(first), pairs_z(second), summed_everywhere(norm_sums)
    first, second, norm_sums, delta_expert_shrink = tie(
        first, second, norm_sums, delta_expert_shrink
    )
    delta_expert_shrink = delta_expert_shrink.T
    first, second = scatter_end(first), scatter_end(second)
    norm_sums = lax.dynamic_slice_in_dim(norm_sums, here * part, part, 1)

    def attention_outputs(pair):
        mine, other = exchange_halves(pair[:part], pair[part:], core)
        both = [jnp.where(core == 0, mine, other), jnp.where(core == 0, other, mine)]
        cut = [[half[:, i * share : (i + 1) * share] for half in both] for i in range(4)]
        project = jnp.concatenate(cut[0] + cut[1] + cut[2], axis=1)
        return project, jnp.concatenate(cut[3], axis=1), mine[:, 4 * share :] + other[:, 4 * share :]

    delta_lower_project, delta_lower_merge, vector_grads = attention_outputs(first)
    delta_upper_project, delta_upper_merge, _ = attention_outputs(third)
    mine, other = exchange_halves(second[:part, :hidden_half], second[part:, :hidden_half], core)
    delta_lower_expand = in_order(mine, other, core, 1)
    mine, other = exchange_halves(
        second[:, hidden_half : hidden_half + width], second[:, hidden_half + width :], core
    )
    both = in_order(mine, other, core, 1)
    delta_lower_shrink = jnp.concatenate(
        [
            jnp.concatenate([both[:, i * share : (i + 1) * share] for i in (row, row + 2)], axis=1)
            for row in range(2)
        ],
        axis=0,
    )
    vector_t = vector_grads.T
    v = [norm_sums[0], norm_sums[1]] + [vector_t[i] for i in range(2, count)]
    delta_lower_expand_bias = vector_t[16:20].reshape(4 * part)
    delta_router_out = vector_grads[:, 32 : 32 + experts]
    delta_expert_shrink_bias = vector_t[64 : 64 + experts]
    return (
        result,
        delta_patches,
        v[0],
        v[1],
        delta_lower_project,
        v[2],
        v[3],
        delta_lower_merge,
        v[4],
        v[5],
        v[6],
        delta_lower_expand,
        delta_lower_expand_bias,
        delta_lower_shrink,
        v[7],
        v[8],
        v[9],
        delta_upper_project,
        v[10],
        v[11],
        delta_upper_merge,
        v[12],
        v[13],
        v[14],
        delta_router_out,
        delta_expert_expand,
        delta_expert_bias,
        delta_expert_shrink,
        delta_expert_shrink_bias,
    )


def solution(mesh):
    groups, parts = mesh.devices.shape
    inner = Mesh(mesh.devices.reshape(groups // 2, 2, parts // 2, 2), ALL)
    dp, seq = ("z", "y"), ("x", "c")
    rows, flat = P(ALL, None), P(ALL)
    in_specs = (
        (rows, P(dp, None), rows)
        + (flat, flat, rows, flat, flat, rows, flat)
        + (flat, flat, rows, flat, rows, flat)
        + (flat, flat, rows, flat, flat, rows, flat)
        + (flat, flat, rows, P(seq, dp), flat, P(dp, seq), P(None, ALL), rows)
    )
    out_specs = (
        (rows, rows)
        + (flat, flat, rows, flat, flat, rows, flat)
        + (flat, flat, rows, flat, rows, flat)
        + (flat, flat, rows, flat, flat, rows, flat)
        + (flat, flat, rows, P(seq, dp), flat, P(dp, seq), P(None, ALL))
    )
    return jax.shard_map(local, mesh=inner, in_specs=in_specs, out_specs=out_specs, check_vma=False)
```

```python
import functools
import math

import jax
import jax.numpy as jnp
from jax import lax
from jax.experimental import pallas as pl
from jax.experimental.pallas import tpu as pltpu
from jax.sharding import Mesh
from jax.sharding import PartitionSpec as P

HEADS = 12
CAP = 17
SLOTS = 24
LONG = 576
EDGE = 192
MASKED = -1000000000.0
EPSILON = 1e-06
LOWTYPE = jnp.bfloat16
WIDE = jnp.float32
ALL = ("z", "y", "x", "c")
CHIPS = ("z", "y", "x")
SWAP = [(0, 1), (1, 0)]


def dot(left, right, dims):
    return lax.dot_general(left, right, ((dims[0], dims[1]), ((), ())), preferred_element_type=WIDE)


def product(left, right):
    return dot(left, right, ((1,), (0,)))


def over_rows(left, right):
    return dot(left, right, ((0,), (0,)))


def over_features(left, right):
    return dot(left, right, ((1,), (1,)))


def low(values):
    return values.astype(LOWTYPE)


def widen(values):
    return values.astype(WIDE)


def swap_cores(values):
    return lax.ppermute(values, "c", SWAP)


def swap_chips(values):
    return lax.ppermute(values, "x", SWAP)


def in_order(mine, other, index, axis):
    first = jnp.where(index == 0, mine, other)
    second = jnp.where(index == 0, other, mine)
    return jnp.concatenate([first, second], axis=axis)


def norm_parts(values):
    center = values - jnp.mean(values, axis=-1, keepdims=True)
    spread = jnp.mean(center * center, axis=-1, keepdims=True)
    return center, lax.rsqrt(spread + EPSILON)


def layer_norm(values, gain, shift):
    center, scale = norm_parts(values)
    return low(center * scale * gain + shift)


def layer_norm_back(values, gain, grad):
    center, scale = norm_parts(values)
    hat = center * scale
    inner = grad * gain
    dvalues = scale * (
        inner
        - jnp.mean(inner, axis=-1, keepdims=True)
        - hat * jnp.mean(inner * hat, axis=-1, keepdims=True)
    )
    return dvalues, jnp.sum(grad * hat, axis=0), jnp.sum(grad, axis=0)


def gelu_parts(values):
    cdf = 0.5 + 0.5 * lax.erf(values * math.sqrt(0.5))
    pdf = jnp.exp(-0.5 * values * values) * (1.0 / math.sqrt(2.0 * math.pi))
    return values * cdf, cdf + values * pdf


def image_of(places, first_end, second_end):
    return (places >= first_end).astype(jnp.int32) + (places >= second_end).astype(jnp.int32)


def attention_places(scalars, rows, halo):
    x = scalars[0]
    edge_start = pl.multiple_of(x * (rows // 2), 64)
    mid_start = pl.multiple_of((1 - x) * (rows - halo), 64)
    mid_place = rows * x + mid_start
    halo_place = rows + x * ((rows - halo) - rows)
    return edge_start, mid_start, rows * x + edge_start, mid_place, halo_place


def edge_mask(place, count, first_end, second_end):
    row = image_of(place + lax.broadcasted_iota(jnp.int32, (count, 1), 0), first_end, second_end)
    column = image_of(place + lax.broadcasted_iota(jnp.int32, (1, count), 1), first_end, second_end)
    return (row == column) & (column != 1)


def mid_mask(mid_place, halo_place, count, first_end, second_end):
    row_places = mid_place + lax.broadcasted_iota(jnp.int32, (count, 1), 0)
    columns = lax.broadcasted_iota(jnp.int32, (1, 2 * count), 1)
    column_places = jnp.where(columns < count, mid_place + columns, halo_place + columns - count)
    row = image_of(row_places, first_end, second_end) == 1
    column = image_of(column_places, first_end, second_end) == 1
    return row & column, row


def lane_of_head(head, dim, lanes):
    lane = lax.broadcasted_iota(jnp.int32, (1, lanes), 1)
    return (lane >= head * dim) & (lane < (head + 1) * dim)


def only(values, lanes):
    return jnp.where(lanes, values, jnp.zeros_like(values))


def attend_kernel(scalars, packed, out, logs, *, rows, halo, dim):
    share = out.shape[1]
    first_end, second_end = scalars[1], scalars[2]
    edge_start, mid_start, edge_place, mid_place, halo_place = attention_places(scalars, rows, halo)
    half = rows // 2
    scale = 1.0 / math.sqrt(dim)
    mask_edge = edge_mask(edge_place, half, first_end, second_end)
    mask_mid, row_mid = mid_mask(mid_place, halo_place, halo, first_end, second_end)

    def one(queries, keys, values, mask):
        total, log_total = None, None
        for head in range(2):
            lanes = lane_of_head(head, dim, 128)
            scores = jnp.where(mask, over_features(only(queries, lanes), keys) * scale, MASKED)
            highest = jnp.max(scores, axis=-1, keepdims=True)
            raised = jnp.exp(scores - highest)
            sums = jnp.sum(raised, axis=-1, keepdims=True)
            weights = low(raised * (1.0 / sums))
            part = product(weights, only(values, lanes))
            total = part if total is None else total + part
            log_sum = highest + jnp.log(sums)
            log_total = log_sum if head == 0 else jnp.where(lanes, log_sum, log_total)
        return total, log_total

    def pair(index, carry):
        query_lanes = pl.ds(pl.multiple_of(index * 128, 128), 128)
        key_lanes = pl.ds(pl.multiple_of(share + index * 128, 128), 128)
        value_lanes = pl.ds(pl.multiple_of(2 * share + index * 128, 128), 128)
        edge = pl.ds(edge_start, half)
        mid = pl.ds(mid_start, halo)
        far = pl.ds(rows, halo)
        result, log_total = one(
            packed[edge, query_lanes], packed[edge, key_lanes], packed[edge, value_lanes], mask_edge
        )
        out[edge, query_lanes] = low(result)
        logs[edge, query_lanes] = log_total
        keys = jnp.concatenate([packed[mid, key_lanes], packed[far, key_lanes]], axis=0)
        values = jnp.concatenate([packed[mid, value_lanes], packed[far, value_lanes]], axis=0)
        result, log_total = one(packed[mid, query_lanes], keys, values, mask_mid)
        out[mid, query_lanes] = jnp.where(row_mid, low(result), out[mid, query_lanes])
        logs[mid, query_lanes] = jnp.where(row_mid, log_total, logs[mid, query_lanes])
        return carry

    lax.fori_loop(0, share // 128, pair, 0)


def attend_back_kernel(scalars, packed, grads, logs, out, *, rows, halo, dim):
    share = grads.shape[1]
    first_end, second_end = scalars[1], scalars[2]
    edge_start, mid_start, edge_place, mid_place, halo_place = attention_places(scalars, rows, halo)
    half = rows // 2
    scale = 1.0 / math.sqrt(dim)
    mask_edge = edge_mask(edge_place, half, first_end, second_end)
    mask_mid, _ = mid_mask(mid_place, halo_place, halo, first_end, second_end)

    def one(queries, keys, values, grad, log_total, mask):
        dquery, dkey, dvalue = None, None, None
        for head in range(2):
            lanes = lane_of_head(head, dim, 128)
            query, key, dout = only(queries, lanes), only(keys, lanes), only(grad, lanes)
            logs_here = log_total[:, head * dim : head * dim + 1]
            scores = jnp.where(mask, over_features(query, keys) * scale, MASKED)
            probs = jnp.exp(scores - logs_here)
            dprobs = over_features(dout, values)
            delta = jnp.sum(probs * dprobs, axis=-1, keepdims=True)
            dscores = low(probs * (dprobs - delta))
            parts = (
                product(dscores, key) * scale,
                over_rows(dscores, query) * scale,
                over_rows(low(probs), dout),
            )
            if head == 0:
                dquery, dkey, dvalue = parts
            else:
                dquery, dkey, dvalue = dquery + parts[0], dkey + parts[1], dvalue + parts[2]
        return low(dquery), low(dkey), low(dvalue)

    out[...] = jnp.zeros_like(out)

    def pair(index, carry):
        query_lanes = pl.ds(pl.multiple_of(index * 128, 128), 128)
        key_lanes = pl.ds(pl.multiple_of(share + index * 128, 128), 128)
        value_lanes = pl.ds(pl.multiple_of(2 * share + index * 128, 128), 128)
        edge = pl.ds(edge_start, half)
        mid = pl.ds(mid_start, halo)
        far = pl.ds(rows, halo)
        dquery, dkey, dvalue = one(
            packed[edge, query_lanes],
            packed[edge, key_lanes],
            packed[edge, value_lanes],
            grads[edge, query_lanes],
            logs[edge, query_lanes],
            mask_edge,
        )
        out[edge, query_lanes] = dquery
        out[edge, key_lanes] = dkey
        out[edge, value_lanes] = dvalue
        keys = jnp.concatenate([packed[mid, key_lanes], packed[far, key_lanes]], axis=0)
        values = jnp.concatenate([packed[mid, value_lanes], packed[far, value_lanes]], axis=0)
        dquery, dkey, dvalue = one(
            packed[mid, query_lanes],
            keys,
            values,
            grads[mid, query_lanes],
            logs[mid, query_lanes],
            mask_mid,
        )
        out[mid, query_lanes] = out[mid, query_lanes] + dquery
        out[mid, key_lanes] = out[mid, key_lanes] + dkey[:halo]
        out[mid, value_lanes] = out[mid, value_lanes] + dvalue[:halo]
        out[far, key_lanes] = dkey[halo:]
        out[far, value_lanes] = dvalue[halo:]
        return carry

    lax.fori_loop(0, share // 128, pair, 0)


def kernel_call(body, outs, operands, flops):
    return pl.pallas_call(
        body,
        out_shape=outs,
        in_specs=[pl.BlockSpec(memory_space=pltpu.SMEM)]
        + [pl.BlockSpec(memory_space=pltpu.VMEM)] * (len(operands) - 1),
        out_specs=[pl.BlockSpec(memory_space=pltpu.VMEM)] * len(outs),
        compiler_params=pltpu.CompilerParams(vmem_limit_bytes=48 * 1024 * 1024),
        cost_estimate=pl.CostEstimate(flops=flops, bytes_accessed=8_000_000, transcendentals=1_700_000),
    )(*operands)


def attend(scalars, packed, rows, halo, dim):
    share = packed.shape[1] // 3
    return kernel_call(
        functools.partial(attend_kernel, rows=rows, halo=halo, dim=dim),
        [jax.ShapeDtypeStruct((rows, share), LOWTYPE), jax.ShapeDtypeStruct((rows, share), WIDE)],
        [scalars, packed],
        1_700_000_000,
    )


def attend_back(scalars, packed, grads, logs, rows, halo, dim):
    [out] = kernel_call(
        functools.partial(attend_back_kernel, rows=rows, halo=halo, dim=dim),
        [jax.ShapeDtypeStruct(packed.shape, LOWTYPE)],
        [scalars, packed, grads, logs],
        4_000_000_000,
    )
    return out


def attention_grads_kernel(normed, dpacked, attended, dmerged, *refs):
    out, width = refs[-1], dmerged.shape[1]
    for i in range(3):
        part = over_rows(normed[...], dpacked[:, i * width : (i + 1) * width])
        out[:, i * width : (i + 1) * width] = low(part)
    out[:, 3 * width : 4 * width] = low(over_rows(attended[...], dmerged[...]))
    if len(refs) == 2:
        out[:, 4 * width :] = low(refs[0][...])


def attention_grads(*operands):
    normed, dpacked, _, dmerged = operands[:4]
    lanes = dpacked.shape[1] + dmerged.shape[1] + sum(o.shape[1] for o in operands[4:])
    inside = pl.BlockSpec(memory_space=pltpu.VMEM)
    return pl.pallas_call(
        attention_grads_kernel,
        out_shape=jax.ShapeDtypeStruct((normed.shape[1], lanes), LOWTYPE),
        in_specs=[inside] * len(operands),
        out_specs=inside,
        compiler_params=pltpu.CompilerParams(vmem_limit_bytes=40 * 1024 * 1024),
        cost_estimate=pl.CostEstimate(
            flops=2 * normed.shape[0] * normed.shape[1] * lanes,
            bytes_accessed=8_000_000,
            transcendentals=0,
        ),
    )(*operands)


def pick(block, index):
    return lax.dynamic_index_in_dim(block, index, 0, keepdims=False)


def xor_pairs(size, flip):
    return [(i, i ^ flip) for i in range(size)]


def assemble_kernel(coords, *refs, parts):
    blocks, outs = refs[: len(refs) - len(parts)], refs[len(refs) - len(parts) :]
    count = blocks[0].shape[0]
    for k, block in enumerate(blocks):
        chip = (coords[0] ^ (k >> 2)) * 4 + (coords[1] ^ ((k >> 1) & 1)) * 2 + (coords[2] ^ (k & 1))
        start = 0
        for out, (width, groups) in zip(outs, parts):
            for group in range(groups):
                place = pl.multiple_of((chip * groups + group) * count, 16)
                out[pl.ds(place, count), :] = block[:, start : start + width]
                start += width


def assemble(coords, blocks, parts):
    count, width = blocks[0].shape
    inside = pl.BlockSpec(memory_space=pltpu.VMEM)
    return pl.pallas_call(
        functools.partial(assemble_kernel, parts=parts),
        out_shape=[
            jax.ShapeDtypeStruct((len(blocks) * count * groups, lanes), LOWTYPE)
            for lanes, groups in parts
        ],
        in_specs=[pl.BlockSpec(memory_space=pltpu.SMEM)] + [inside] * len(blocks),
        out_specs=[inside] * len(parts),
        compiler_params=pltpu.CompilerParams(vmem_limit_bytes=40 * 1024 * 1024),
        cost_estimate=pl.CostEstimate(
            flops=0, bytes_accessed=4 * len(blocks) * count * width, transcendentals=0
        ),
    )(coords, *blocks)


def tie(*values):
    return lax.optimization_barrier(values)


def gather_z(pair, after=()):
    if lax.axis_size("z") != 4:
        return [lax.all_gather(pair, CHIPS, axis=0, tiled=True), pair]
    if after:
        pair, after = tie(pair, after)
    return [pair] + [lax.ppermute(pair, "z", xor_pairs(4, k)) for k in (1, 2, 3)]


def gather_plane(along):
    if lax.axis_size("z") != 4:
        return []
    return [(swap_chips(here), lax.ppermute(here, "y", SWAP)) for here in along]


def gather_end(along, plane, parts, x_first):
    if lax.axis_size("z") != 4:
        whole, count = along[0], along[1].shape[0]
        outs, start = [], 0
        for lanes, groups in parts:
            piece = whole[:, start : start + lanes * groups]
            piece = piece.reshape(-1, count, groups, lanes).transpose(0, 2, 1, 3)
            outs.append(piece.reshape(-1, lanes))
            start += lanes * groups
        return outs, ()
    blocks, across = [], []
    for k, (here, (by_x, by_y)) in enumerate(zip(along, plane)):
        if k in x_first:
            blocks += [here, by_x, by_y, lax.ppermute(by_x, "y", SWAP)]
            across += [by_x]
        else:
            blocks += [here, by_x, by_y, swap_chips(by_y)]
            across += [by_x, blocks[-1]]
    coords = jnp.stack([lax.axis_index(name) for name in CHIPS]).astype(jnp.int32)
    return assemble(coords, blocks, parts), tuple(across)


def added(left, right):
    return low(widen(left) + widen(right))


def at(values, index, axis):
    return lax.dynamic_index_in_dim(values, index, axis, keepdims=False)


def pairs_first(grads):
    if lax.axis_size("z") != 4:
        return lax.psum_scatter(low(grads), CHIPS, scatter_dimension=0, tiled=True)
    z, y, x = [lax.axis_index(name) for name in CHIPS]
    view = low(grads).reshape(2, 2, 2, 2, grads.shape[0] // 16, grads.shape[1])
    near, far = at(view, z // 2, 0), at(view, 1 - z // 2, 0)
    from_y, from_x = lax.ppermute(at(near, 1 - y, 1), "y", SWAP), swap_chips(at(far, 1 - x, 2))
    return at(near, y, 1), from_y, at(far, x, 2), from_x


def pairs_second(state):
    if lax.axis_size("z") != 4:
        return state
    y, x = lax.axis_index("y"), lax.axis_index("x")
    near, far = added(*state[:2]), added(*state[2:])
    from_x, from_y = swap_chips(at(near, 1 - x, 1)), lax.ppermute(at(far, 1 - y, 1), "y", SWAP)
    return at(near, x, 1), from_x, at(far, y, 1), from_y


def pairs_z(state):
    if lax.axis_size("z") != 4:
        return state
    low_bit = lax.axis_index("z") % 2
    near, far = added(*state[:2]), added(*state[2:])
    sent = (at(near, 1 - low_bit, 0), at(far, low_bit, 0), at(far, 1 - low_bit, 0))
    got = [lax.ppermute(piece, "z", xor_pairs(4, k + 1)) for k, piece in enumerate(sent)]
    return [at(near, low_bit, 0)] + got


def summed_everywhere(values):
    if lax.axis_size("z") != 4:
        return lax.psum(values, ALL)
    for name, pairs in (("c", SWAP), ("x", SWAP), ("y", SWAP), ("z", xor_pairs(4, 1)), ("z", xor_pairs(4, 2))):
        values = values + lax.ppermute(values, name, pairs)
    return values


def scatter_y(grads):
    if lax.axis_size("z") != 4:
        return lax.psum_scatter(low(grads), CHIPS, scatter_dimension=0, tiled=True)
    y = lax.axis_index("y")
    view = low(grads).reshape(4, 2, 2, grads.shape[0] // 16, grads.shape[1])
    return at(view, y, 1), lax.ppermute(at(view, 1 - y, 1), "y", SWAP)


def scatter_x(state):
    if lax.axis_size("z") != 4:
        return state
    x, values = lax.axis_index("x"), added(*state)
    return at(values, x, 1), swap_chips(at(values, 1 - x, 1))


def scatter_z(state):
    if lax.axis_size("z") != 4:
        return state
    z, values = lax.axis_index("z"), added(*state)
    sent = [lax.ppermute(at(values, z ^ k, 0), "z", xor_pairs(4, k)) for k in (1, 2, 3)]
    return [at(values, z, 0)] + sent


def scatter_end(state):
    if lax.axis_size("z") != 4:
        return widen(state)
    return widen(state[0]) + widen(state[1]) + widen(state[2]) + widen(state[3])


def exchange_halves(first, second, core):
    mine = jnp.where(core == 0, first, second)
    other = widen(swap_cores(low(jnp.where(core == 0, second, first))))
    return mine, other


def cut_kernel(place, weight, *outs):
    for k, out in enumerate(outs):

        @pl.when(pl.program_id(0) == k)
        def _(out=out):
            out[...] = low(weight[...])


def cut_columns(weight, place):
    rows, units = weight.shape[0], weight.shape[1] // 4
    return pl.pallas_call(
        cut_kernel,
        grid_spec=pltpu.PrefetchScalarGridSpec(
            num_scalar_prefetch=1,
            grid=(4,),
            in_specs=[pl.BlockSpec((rows, units), lambda i, p: (0, p[0] ^ i))],
            out_specs=[pl.BlockSpec((rows, units), lambda i, p: (0, 0))] * 4,
        ),
        out_shape=[jax.ShapeDtypeStruct((rows, units), LOWTYPE)] * 4,
        compiler_params=pltpu.CompilerParams(vmem_limit_bytes=32 * 1024 * 1024),
        cost_estimate=pl.CostEstimate(flops=0, bytes_accessed=6 * weight.size, transcendentals=0),
    )(place, weight)


def stack_kernel(place, *refs):
    blocks, out = refs[:4], refs[4]
    count = blocks[0].shape[0]
    for k, block in enumerate(blocks):
        out[pl.ds(pl.multiple_of((place[0] ^ k) * count, 16), count), :] = block[...]


def stack_rows(place, blocks):
    count, width = blocks[0].shape
    inside = pl.BlockSpec(memory_space=pltpu.VMEM)
    return pl.pallas_call(
        stack_kernel,
        out_shape=jax.ShapeDtypeStruct((4 * count, width), LOWTYPE),
        in_specs=[pl.BlockSpec(memory_space=pltpu.SMEM)] + [inside] * 4,
        out_specs=inside,
        compiler_params=pltpu.CompilerParams(vmem_limit_bytes=32 * 1024 * 1024),
        cost_estimate=pl.CostEstimate(flops=0, bytes_accessed=16 * count * width, transcendentals=0),
    )(place, *blocks)


def join_kernel(place, *refs):
    for k in range(4):

        @pl.when(pl.program_id(0) == k)
        def _(k=k):
            refs[4][...] = widen(refs[k][...])


def join_columns(place, pieces):
    rows, units = pieces[0].shape
    return pl.pallas_call(
        join_kernel,
        grid_spec=pltpu.PrefetchScalarGridSpec(
            num_scalar_prefetch=1,
            grid=(4,),
            in_specs=[pl.BlockSpec((rows, units), lambda i, p: (0, 0))] * 4,
            out_specs=pl.BlockSpec((rows, units), lambda i, p: (0, p[0] ^ i)),
        ),
        out_shape=jax.ShapeDtypeStruct((rows, 4 * units), WIDE),
        compiler_params=pltpu.CompilerParams(vmem_limit_bytes=40 * 1024 * 1024),
        cost_estimate=pl.CostEstimate(flops=0, bytes_accessed=24 * rows * units, transcendentals=0),
    )(place, *pieces)


def column_sums(values):
    return product(jnp.ones((8, values.shape[0]), LOWTYPE), values)[0]


def halves_of(weight, width):
    parts = [weight[:, i : i + width] for i in range(0, weight.shape[1], width)]
    return tuple(
        jnp.concatenate([p[:, h * width // 2 : (h + 1) * width // 2] for p in parts], axis=1)
        for h in range(2)
    )


def cut_dense(project, merge, small, expand, shrink, upper_project, upper_merge):
    width = merge.shape[1]
    half_rows = shrink.shape[0] // 2
    project, merge = halves_of(project, width), halves_of(merge, width)
    upper_project, upper_merge = halves_of(upper_project, width), halves_of(upper_merge, width)
    expand, shrink = halves_of(expand, expand.shape[1]), halves_of(shrink, width)
    return [
        (
            jnp.concatenate([project[h], merge[h], small], axis=1),
            jnp.concatenate([expand[h], upper_project[h], upper_merge[h]], axis=1),
            jnp.concatenate([shrink[h][:half_rows], shrink[h][half_rows:]], axis=1),
        )
        for h in range(2)
    ]


def prologue_kernel(core, *refs, count):
    operands = count + 9
    sources, outs = refs[:operands], refs[operands : operands + 6]
    table, small, sems = refs[operands + 6 : operands + 9]
    inside = refs[operands + 9 :]
    copies = [
        pltpu.make_async_copy(source, target, sems.at[i])
        for i, (source, target) in enumerate(zip(sources, inside))
    ]
    for copy in copies:
        copy.start()
    for copy in copies:
        copy.wait()
    vectors, (expand_bias, router, bias), weights = inside[:count], inside[count : count + 3], inside[count + 3 :]
    part = router.shape[0]
    table[...] = jnp.zeros_like(table)
    for i, vector in enumerate(vectors):
        table[i : i + 1, 0:part] = vector[...].reshape(1, part)
    biases = expand_bias[...].reshape(1, 4 * part)
    for q in range(4):
        table[16 + q : 17 + q, 0:part] = biases[:, q * part : (q + 1) * part]
    small[...] = table[...].T
    small[0:part, 32 : 32 + router.shape[1]] = router[...]
    small[0:part, 64 : 64 + bias.shape[1]] = bias[...]
    values = [ref[...] for ref in weights]
    cut = cut_dense(values[0], values[1], small[0:part, :], *values[2:])
    first = core[0] == 0
    for i in range(3):
        outs[i][...] = low(jnp.where(first, cut[0][i], cut[1][i]))
        outs[3 + i][...] = low(jnp.where(first, cut[1][i], cut[0][i]))


def prologue(core, vectors, expand_bias, router, bias, weights):
    part = router.shape[0]
    if lax.axis_size("z") != 4:
        rows = [jnp.stack(vectors), jnp.zeros((16 - len(vectors), part), WIDE)]
        rows += [expand_bias.reshape(4, part), jnp.zeros((12, part), WIDE)]
        small = jnp.concatenate([jnp.concatenate(rows).T, router, bias], axis=1)
        small = jnp.pad(small, ((0, 0), (0, 128 - small.shape[1])))
        cut = cut_dense(weights[0], weights[1], small, *weights[2:])
        picked = [[jnp.where(core == h, a, b) for a, b in zip(*cut)] for h in range(2)]
        return [low(v) for v in picked[0]], [low(v) for v in picked[1]]
    lanes = [weights[0].shape[1] // 2 + weights[1].shape[1] // 2 + 128]
    lanes += [sum(w.shape[1] // 2 for w in (weights[2], weights[4], weights[5]))]
    shapes = [(part, lanes[0]), (part, lanes[1]), (weights[3].shape[0] // 2, weights[3].shape[1])]
    inside = pl.BlockSpec(memory_space=pltpu.VMEM)
    operands = [*vectors, expand_bias, router, bias, *weights]
    outs = pl.pallas_call(
        functools.partial(prologue_kernel, count=len(vectors)),
        out_shape=[jax.ShapeDtypeStruct(shape, LOWTYPE) for shape in shapes * 2],
        in_specs=[pl.BlockSpec(memory_space=pltpu.SMEM)]
        + [pl.BlockSpec(memory_space=pl.ANY)] * len(operands),
        out_specs=[inside] * 6,
        scratch_shapes=[
            pltpu.VMEM((128, 128), WIDE),
            pltpu.VMEM((128, 128), WIDE),
            pltpu.SemaphoreType.DMA((len(operands),)),
        ]
        + [pltpu.VMEM(operand.shape, WIDE) for operand in operands],
        compiler_params=pltpu.CompilerParams(vmem_limit_bytes=60 * 1024 * 1024),
        cost_estimate=pl.CostEstimate(flops=0, bytes_accessed=2_500_000, transcendentals=0),
    )(core.reshape(1).astype(jnp.int32), *operands)
    return outs[:3], outs[3:]


def local(
    patches,
    image_lengths,
    expert_ids,
    lower_norm_gain,
    lower_norm_shift,
    lower_project,
    lower_query_bias,
    lower_value_bias,
    lower_merge,
    lower_merge_bias,
    lower_second_gain,
    lower_second_shift,
    lower_expand,
    lower_expand_bias,
    lower_shrink,
    lower_shrink_bias,
    upper_norm_gain,
    upper_norm_shift,
    upper_project,
    upper_query_bias,
    upper_value_bias,
    upper_merge,
    upper_merge_bias,
    upper_second_gain,
    upper_second_shift,
    router,
    expert_expand,
    expert_expand_bias,
    expert_shrink,
    expert_shrink_bias,
    output_grad,
):
    x, core = lax.axis_index("x"), lax.axis_index("c")
    devices = lax.axis_size(ALL)
    here = lax.axis_index(ALL)
    own, width = patches.shape
    rows = 2 * own
    dim = width // HEADS
    halo = rows - EDGE
    share = width // 2
    experts = router.shape[1]
    copies = devices // experts
    slots = experts * SLOTS
    part = lower_norm_gain.shape[0]
    lengths = image_lengths[0]
    scalars = jnp.stack([x, lengths[0], lengths[0] + lengths[1]]).astype(jnp.int32)
    mid_start = (1 - x) * (rows - halo)

    def halo_rows(full):
        count = halo // 2
        piece = lax.dynamic_slice_in_dim(full, mid_start + core * count, count, 0)
        got = swap_chips(piece)
        return in_order(got, swap_cores(got), core, 0)

    vectors = [
        lower_norm_gain,
        lower_norm_shift,
        lower_query_bias,
        lower_value_bias,
        lower_merge_bias,
        lower_second_gain,
        lower_second_shift,
        lower_shrink_bias,
        upper_norm_gain,
        upper_norm_shift,
        upper_query_bias,
        upper_value_bias,
        upper_merge_bias,
        upper_second_gain,
        upper_second_shift,
    ]
    count = len(vectors)
    shares, others = prologue(
        core,
        vectors,
        lower_expand_bias,
        router,
        expert_shrink_bias.T,
        [lower_project, lower_merge, lower_expand, lower_shrink, upper_project, upper_merge],
    )
    got = [swap_cores(other) for other in others]
    pair_1 = in_order(shares[0], got[0], core, 0)
    hidden_half = lower_expand.shape[1] // 2
    pair_2 = in_order(shares[1], got[1], core, 0)
    pair_3 = pair_2[:, hidden_half:]
    pair_2 = jnp.concatenate(
        [pair_2[:, :hidden_half], in_order(shares[2], got[2], core, 1)], axis=1
    )
    along_1 = gather_z(pair_1)
    (lower_project_c, lower_merge_c, table), _ = gather_end(
        along_1, gather_plane(along_1), ((3 * share, 1), (share, 1), (128, 1)), (0, 2)
    )
    seat = (2 * x + core).reshape(1).astype(jnp.int32)
    expand_cut, shrink_cut = cut_columns(expert_expand, seat), cut_columns(expert_shrink.T, seat)
    table, expand_cut, shrink_cut = lax.optimization_barrier((table, expand_cut, shrink_cut))
    along_2 = gather_z(pair_2, tuple(along_1[1:2]))
    (expand_c, shrink_half), crossed = gather_end(
        along_2, gather_plane(along_2), ((hidden_half, 1), (share, 4)), (0, 2)
    )
    upper_c = lax.all_gather(pair_3, CHIPS, axis=0, tiled=True)
    upper_project_c, upper_merge_c = upper_c[:, : 3 * share], upper_c[:, 3 * share :]
    lower_merge_full = in_order(lower_merge_c, swap_cores(lower_merge_c), core, 1)
    shrink_parts = shrink_half.reshape(2, hidden_half, share)
    shrink_c = in_order(pick(shrink_parts, core), swap_cores(pick(shrink_parts, 1 - core)), core, 1)
    table_t = table.T
    wide_t = widen(table_t[:32])
    (
        ln1_gain,
        ln1_shift,
        lower_qb,
        lower_vb,
        lower_mb,
        ln2_gain,
        ln2_shift,
        shrink_b,
        ln3_gain,
        ln3_shift,
        upper_qb,
        upper_vb,
        upper_mb,
        ln4_gain,
        ln4_shift,
    ) = [wide_t[i] for i in range(count)]
    expand_b = wide_t[16:20].reshape(4, devices, part).transpose(1, 0, 2).reshape(2, hidden_half)
    expand_b = pick(expand_b, core)
    router_w = table[:, 32 : 32 + experts]
    router_t = table_t[32 : 32 + experts]
    expert_bias = table_t[64 : 64 + experts]

    def between(values, k):
        return lax.ppermute(values, ("x", "c"), xor_pairs(4, k))

    def whole_expert(pieces):
        if crossed:
            pieces, _ = lax.optimization_barrier((pieces, crossed))
        across = between(pieces[2], 2)
        last, _ = tie(pieces[3], across)
        return [pieces[0], between(pieces[1], 1), across, between(last, 3)]

    def expert_parts(grads):
        count = grads.shape[0] // 4
        pieces = [
            lax.dynamic_slice_in_dim(grads, (seat[0] ^ k) * count, count, 0) for k in range(4)
        ]
        far_piece = between(pieces[2], 2)
        last, _ = tie(pieces[3], far_piece)
        return [pieces[0], between(pieces[1], 1), far_piece, between(last, 3)]

    expand_e = whole_expert(expand_cut)
    shrink_e = whole_expert(shrink_cut)

    order = lax.broadcasted_iota(jnp.int32, (own, own), 0)
    before_it = low(order > lax.broadcasted_iota(jnp.int32, (own, own), 1))
    chosen = [
        low(expert_ids[:, k : k + 1] == jnp.arange(experts, dtype=jnp.int32)[None]) for k in range(2)
    ]
    earlier = product(before_it, chosen[0] + chosen[1])
    places = [
        expert_ids[:, k] * SLOTS
        + jnp.sum(widen(chosen[k]) * earlier, axis=1).astype(jnp.int32)
        for k in range(2)
    ]
    placed = [
        low(place[:, None] == jnp.arange(slots, dtype=jnp.int32)[None]) for place in places
    ]
    placed_any = placed[0] + placed[1]

    def to_experts(values):
        sent = low(over_rows(placed_any, values)).reshape(experts, SLOTS, width)
        if copies > 1:
            sent = jnp.repeat(sent, copies, axis=0)
        got = lax.all_to_all(sent, ALL, 0, 0, tiled=True)
        return got.reshape(devices * SLOTS, width)

    def to_patches(values):
        got = lax.all_to_all(low(values).reshape(devices, SLOTS, width), ALL, 0, 0, tiled=True)
        if copies > 1:
            got = low(jnp.sum(widen(got.reshape(experts, copies, SLOTS, width)), axis=1))
        return got.reshape(slots, width)

    grads_sent = low(output_grad)

    full = in_order(patches, swap_cores(patches), core, 0)
    x0 = widen(full)

    def half(vector):
        return lax.dynamic_slice_in_dim(vector, core * share, share, 0)

    def attention_forward(residual, normed, project_c, query_bias, value_bias):
        bias = jnp.concatenate([half(query_bias), jnp.zeros((share,), WIDE), half(value_bias)])
        packed = low(product(normed, project_c) + bias)
        attended, logs = attend(scalars, packed, rows, halo, dim)
        attended_full = in_order(attended, swap_cores(attended), core, 1)
        return packed, logs, attended_full

    a1 = layer_norm(jnp.concatenate([x0, widen(halo_rows(full))], axis=0), ln1_gain, ln1_shift)
    packed1, logs1, attended1 = attention_forward(x0, a1, lower_project_c, lower_qb, lower_vb)
    x1 = x0 + product(attended1, lower_merge_full) + lower_mb

    b = layer_norm(x1, ln2_gain, ln2_shift)
    pre = product(b, expand_c) + expand_b
    hidden = low(gelu_parts(pre)[0])
    upper_merge_full = in_order(upper_merge_c, swap_cores(upper_merge_c), core, 1)
    hidden_full = in_order(hidden, swap_cores(hidden), core, 1)
    partial = low(product(hidden, shrink_c))
    x2 = x1 + (widen(partial) + widen(swap_cores(partial))) + shrink_b

    a2_own = layer_norm(x2, ln3_gain, ln3_shift)
    a2 = jnp.concatenate([a2_own, halo_rows(a2_own)], axis=0)
    a2, expand_e[2] = tie(a2, expand_e[2])
    packed2, logs2, attended2 = attention_forward(x2, a2, upper_project_c, upper_qb, upper_vb)

    attended2, expand_e[3], grad_rows = tie(attended2, expand_e[3], to_experts(grads_sent))

    def own_rows(values):
        return lax.dynamic_slice_in_dim(values, core * own, own, 0)

    x3 = own_rows(x2) + product(own_rows(attended2), upper_merge_full) + upper_mb
    normed = layer_norm(x3, ln4_gain, ln4_shift)
    rows_in = to_experts(normed)
    rows_in, expand_e, shrink_e[2] = tie(rows_in, expand_e, shrink_e[2])
    expand_e, shrink_e = stack_rows(seat, expand_e), stack_rows(seat, shrink_e)

    def gating(values):
        logits = product(values, router_w)
        raised = jnp.exp(logits - jnp.max(logits, axis=1, keepdims=True))
        return raised / jnp.sum(raised, axis=1, keepdims=True)

    mine = (jnp.arange(experts, dtype=jnp.int32) == here // copies).astype(WIDE)[None]
    probs_in = gating(rows_in)
    gate_in = jnp.sum(probs_in * mine, axis=1, keepdims=True)
    raw = product(grad_rows, shrink_e)
    before = product(rows_in, expand_e) + expert_expand_bias.astype(LOWTYPE).astype(WIDE)
    expert_hidden, slope = gelu_parts(before)
    expert_hidden = low(expert_hidden)
    once = (here % copies == 0).astype(WIDE)
    bias_here = product(low(mine), expert_bias) * once
    delta_gate = jnp.sum(widen(expert_hidden) * raw, axis=1, keepdims=True)
    delta_gate = delta_gate + jnp.sum(widen(grad_rows) * bias_here, axis=1, keepdims=True)
    dbefore = low(gate_in * raw * slope)
    dlogits = low(probs_in * delta_gate * (mine - gate_in))
    drows = over_features(dbefore, expand_e) + product(dlogits, router_t)
    drows, dbefore, expert_hidden = tie(low(drows), dbefore, expert_hidden)
    returned_grad = to_patches(drows)
    returned = to_patches(over_features(expert_hidden, shrink_e))
    g_out = low(gate_in * widen(grad_rows))
    delta_expand_e = over_rows(rows_in, dbefore)
    delta_shrink_e = over_rows(g_out, expert_hidden)
    delta_expert_bias = column_sums(dbefore)
    delta_router = over_rows(rows_in, dlogits)
    delta_shrink_e = low(delta_shrink_e)
    expand_pieces = expert_parts(low(delta_expand_e))
    returned_grad, expand_pieces[1], delta_shrink_e = tie(
        returned_grad, expand_pieces[1], delta_shrink_e
    )
    delta_shrink_bias = (column_sums(g_out) * once)[:, None] * mine

    delta_normed = product(placed_any, returned_grad)
    dx3, dgain4, dshift4 = layer_norm_back(x3, ln4_gain, delta_normed)
    dx3 = output_grad + dx3
    dx3 = in_order(dx3, swap_cores(dx3), core, 0)
    dx3, expand_pieces[2] = tie(dx3, expand_pieces[2])
    half_lanes = (jnp.arange(width, dtype=jnp.int32) // share == core).astype(WIDE)

    def columns_of_half(values):
        return lax.dynamic_slice_in_dim(values, core * share, share, 1)

    def spread(vector):
        return lax.dynamic_update_slice_in_dim(jnp.zeros((width,), WIDE), vector, core * share, 0)

    def attention_backward(
        dresidual, residual, normed, packed, logs, attended, gain, project_c, merge, waiting
    ):
        dmerged = low(dresidual)
        delta_merge_bias = column_sums(dmerged) * half_lanes
        merge_rows = lax.dynamic_slice_in_dim(merge, core * share, share, 0)
        dattended = low(over_features(dmerged, merge_rows))
        dpacked = attend_back(scalars, packed, dattended, logs, rows, halo, dim)
        dnormed = over_features(dpacked, project_c)
        dnormed, waiting = tie(dnormed, waiting)
        far = swap_chips(low(dnormed[rows:]))
        bias_sums = column_sums(dpacked)
        mine_part = low(
            dnormed[:rows]
            + lax.dynamic_update_slice_in_dim(jnp.zeros((rows, width), WIDE), widen(far), mid_start, 0)
        )
        dnormed = widen(mine_part) + widen(swap_cores(mine_part))
        dinput, dgain, dshift = layer_norm_back(residual, gain, dnormed)
        sums = (
            dgain * half_lanes,
            dshift * half_lanes,
            spread(bias_sums[:share]),
            spread(bias_sums[2 * share :]),
            delta_merge_bias,
        )
        outs = dresidual + dinput, (normed, dpacked, attended, columns_of_half(dmerged)), sums, far
        return *outs, waiting

    dx2, upper_grads, upper_sums, far, expand_pieces[3] = attention_backward(
        dx3,
        x2,
        a2,
        packed2,
        logs2,
        attended2,
        ln3_gain,
        upper_project_c,
        upper_merge_full,
        expand_pieces[3],
    )
    delta_shrink_e, _ = tie(delta_shrink_e, far)
    shrink_pieces = expert_parts(delta_shrink_e)
    third = scatter_y(attention_grads(*upper_grads))

    dmlp = low(dx2)
    delta_shrink_b = column_sums(dmlp) * half_lanes
    delta_shrink = low(over_rows(hidden_full, columns_of_half(dmlp)))
    delta_shrink = delta_shrink.reshape(-1, 4, 2 * part, share).transpose(0, 2, 1, 3)
    dpre = low(over_features(dmlp, shrink_c) * gelu_parts(pre)[1])
    dpre, shrink_pieces[2] = tie(dpre, shrink_pieces[2])
    dnormed = low(over_features(dpre, expand_c))
    delta_expand = low(over_rows(b, dpre))
    delta_expand_b = column_sums(dpre)
    second = pairs_first(
        jnp.concatenate([delta_expand, delta_shrink.reshape(width, 4 * share)], axis=1)
    )
    dinput, dgain2, dshift2 = layer_norm_back(x1, ln2_gain, widen(dnormed) + widen(swap_cores(dnormed)))
    dx1 = dx2 + dinput
    dx1, third, returned = tie(dx1, third, returned)
    third = scatter_x(third)

    dx0, lower_grads, lower_sums, _, (third, second, shrink_pieces[3]) = attention_backward(
        dx1,
        x0,
        a1,
        packed1,
        logs1,
        attended1,
        ln1_gain,
        lower_project_c,
        lower_merge_full,
        (third, second, shrink_pieces[3]),
    )
    second = pairs_second(second)
    third = scatter_z(third)
    dx0, returned = tie(dx0, returned)
    probs = gating(normed)
    result = x3
    for k in range(2):
        gate = jnp.sum(widen(chosen[k]) * probs, axis=1, keepdims=True)
        picked = product(placed[k], returned) + product(chosen[k], expert_bias)
        result = result + gate * picked

    delta_patches = own_rows(dx0)

    expand_sums = lax.dynamic_update_slice_in_dim(
        jnp.zeros((2 * hidden_half,), WIDE), delta_expand_b, core * hidden_half, 0
    )
    expand_sums = expand_sums.reshape(devices, 4, part).transpose(1, 0, 2).reshape(4, width)
    sums = jnp.concatenate(
        [
            jnp.stack(
                [jnp.zeros((width,), WIDE)] * 2
                + list(lower_sums[2:])
                + [dgain2 * half_lanes, dshift2 * half_lanes, delta_shrink_b]
                + list(upper_sums)
                + [dgain4, dshift4, jnp.zeros((width,), WIDE)]
            ),
            expand_sums,
            jnp.zeros((12, width), WIDE),
        ]
    )
    small_grads = jnp.concatenate([sums.T, delta_router, delta_shrink_bias], axis=1)
    small_grads = jnp.pad(small_grads, ((0, 0), (0, 128 - small_grads.shape[1])))
    first = pairs_first(attention_grads(*lower_grads, small_grads))
    first, third, expand_pieces, shrink_pieces = tie(first, third, expand_pieces, shrink_pieces)
    third = scatter_end(third)
    delta_expert_expand = join_columns(seat, expand_pieces)
    delta_expert_shrink = join_columns(seat, shrink_pieces)
    norm_sums = jnp.concatenate([jnp.stack(lower_sums[:2]), jnp.zeros((6, width), WIDE)])
    first, second, norm_sums, delta_expert_expand = tie(
        pairs_second(first), second, norm_sums, delta_expert_expand
    )
    first, second, norm_sums = pairs_z(first), pairs_z(second), summed_everywhere(norm_sums)
    first, second, norm_sums, delta_expert_shrink = tie(
        first, second, norm_sums, delta_expert_shrink
    )
    delta_expert_shrink = delta_expert_shrink.T
    first, second = scatter_end(first), scatter_end(second)
    norm_sums = lax.dynamic_slice_in_dim(norm_sums, here * part, part, 1)

    def attention_outputs(pair):
        mine, other = exchange_halves(pair[:part], pair[part:], core)
        both = [jnp.where(core == 0, mine, other), jnp.where(core == 0, other, mine)]
        cut = [[half[:, i * share : (i + 1) * share] for half in both] for i in range(4)]
        project = jnp.concatenate(cut[0] + cut[1] + cut[2], axis=1)
        return project, jnp.concatenate(cut[3], axis=1), mine[:, 4 * share :] + other[:, 4 * share :]

    delta_lower_project, delta_lower_merge, vector_grads = attention_outputs(first)
    delta_upper_project, delta_upper_merge, _ = attention_outputs(third)
    mine, other = exchange_halves(second[:part, :hidden_half], second[part:, :hidden_half], core)
    delta_lower_expand = in_order(mine, other, core, 1)
    mine, other = exchange_halves(
        second[:, hidden_half : hidden_half + width], second[:, hidden_half + width :], core
    )
    both = in_order(mine, other, core, 1)
    delta_lower_shrink = jnp.concatenate(
        [
            jnp.concatenate([both[:, i * share : (i + 1) * share] for i in (row, row + 2)], axis=1)
            for row in range(2)
        ],
        axis=0,
    )
    vector_t = vector_grads.T
    v = [norm_sums[0], norm_sums[1]] + [vector_t[i] for i in range(2, count)]
    delta_lower_expand_bias = vector_t[16:20].reshape(4 * part)
    delta_router_out = vector_grads[:, 32 : 32 + experts]
    delta_expert_shrink_bias = vector_t[64 : 64 + experts]
    return (
        result,
        delta_patches,
        v[0],
        v[1],
        delta_lower_project,
        v[2],
        v[3],
        delta_lower_merge,
        v[4],
        v[5],
        v[6],
        delta_lower_expand,
        delta_lower_expand_bias,
        delta_lower_shrink,
        v[7],
        v[8],
        v[9],
        delta_upper_project,
        v[10],
        v[11],
        delta_upper_merge,
        v[12],
        v[13],
        v[14],
        delta_router_out,
        delta_expert_expand,
        delta_expert_bias,
        delta_expert_shrink,
        delta_expert_shrink_bias,
    )


def solution(mesh):
    groups, parts = mesh.devices.shape
    inner = Mesh(mesh.devices.reshape(groups // 2, 2, parts // 2, 2), ALL)
    dp, seq = ("z", "y"), ("x", "c")
    rows, flat = P(ALL, None), P(ALL)
    in_specs = (
        (rows, P(dp, None), rows)
        + (flat, flat, rows, flat, flat, rows, flat)
        + (flat, flat, rows, flat, rows, flat)
        + (flat, flat, rows, flat, flat, rows, flat)
        + (flat, flat, rows, P(seq, dp), flat, P(dp, seq), P(None, ALL), rows)
    )
    out_specs = (
        (rows, rows)
        + (flat, flat, rows, flat, flat, rows, flat)
        + (flat, flat, rows, flat, rows, flat)
        + (flat, flat, rows, flat, flat, rows, flat)
        + (flat, flat, rows, P(seq, dp), flat, P(dp, seq), P(None, ALL))
    )
    return jax.shard_map(local, mesh=inner, in_specs=in_specs, out_specs=out_specs, check_vma=False)
```

```python
import functools
import math

import jax
import jax.numpy as jnp
from jax import lax
from jax.experimental import pallas as pl
from jax.experimental.pallas import tpu as pltpu
from jax.sharding import Mesh
from jax.sharding import PartitionSpec as P

HEADS = 12
CAP = 17
SLOTS = 24
LONG = 576
EDGE = 192
MASKED = -1000000000.0
EPSILON = 1e-06
LOWTYPE = jnp.bfloat16
WIDE = jnp.float32
ALL = ("z", "y", "x", "c")
CHIPS = ("z", "y", "x")
SWAP = [(0, 1), (1, 0)]


def dot(left, right, dims):
    return lax.dot_general(left, right, ((dims[0], dims[1]), ((), ())), preferred_element_type=WIDE)


def product(left, right):
    return dot(left, right, ((1,), (0,)))


def over_rows(left, right):
    return dot(left, right, ((0,), (0,)))


def over_features(left, right):
    return dot(left, right, ((1,), (1,)))


def low(values):
    return values.astype(LOWTYPE)


def widen(values):
    return values.astype(WIDE)


def swap_cores(values):
    return lax.ppermute(values, "c", SWAP)


def swap_chips(values):
    return lax.ppermute(values, "x", SWAP)


def in_order(mine, other, index, axis):
    first = jnp.where(index == 0, mine, other)
    second = jnp.where(index == 0, other, mine)
    return jnp.concatenate([first, second], axis=axis)


def norm_parts(values):
    center = values - jnp.mean(values, axis=-1, keepdims=True)
    spread = jnp.mean(center * center, axis=-1, keepdims=True)
    return center, lax.rsqrt(spread + EPSILON)


def layer_norm(values, gain, shift):
    center, scale = norm_parts(values)
    return low(center * scale * gain + shift)


def layer_norm_back(values, gain, grad):
    center, scale = norm_parts(values)
    hat = center * scale
    inner = grad * gain
    dvalues = scale * (
        inner
        - jnp.mean(inner, axis=-1, keepdims=True)
        - hat * jnp.mean(inner * hat, axis=-1, keepdims=True)
    )
    return dvalues, jnp.sum(grad * hat, axis=0), jnp.sum(grad, axis=0)


def gelu_parts(values):
    cdf = 0.5 + 0.5 * lax.erf(values * math.sqrt(0.5))
    pdf = jnp.exp(-0.5 * values * values) * (1.0 / math.sqrt(2.0 * math.pi))
    return values * cdf, cdf + values * pdf


def image_of(places, first_end, second_end):
    return (places >= first_end).astype(jnp.int32) + (places >= second_end).astype(jnp.int32)


def attention_places(scalars, rows, halo):
    x = scalars[0]
    edge_start = pl.multiple_of(x * (rows // 2), 64)
    mid_start = pl.multiple_of((1 - x) * (rows - halo), 64)
    mid_place = rows * x + mid_start
    halo_place = rows + x * ((rows - halo) - rows)
    return edge_start, mid_start, rows * x + edge_start, mid_place, halo_place


def edge_mask(place, count, first_end, second_end):
    row = image_of(place + lax.broadcasted_iota(jnp.int32, (count, 1), 0), first_end, second_end)
    column = image_of(place + lax.broadcasted_iota(jnp.int32, (1, count), 1), first_end, second_end)
    return (row == column) & (column != 1)


def mid_mask(mid_place, halo_place, count, first_end, second_end):
    row_places = mid_place + lax.broadcasted_iota(jnp.int32, (count, 1), 0)
    columns = lax.broadcasted_iota(jnp.int32, (1, 2 * count), 1)
    column_places = jnp.where(columns < count, mid_place + columns, halo_place + columns - count)
    row = image_of(row_places, first_end, second_end) == 1
    column = image_of(column_places, first_end, second_end) == 1
    return row & column, row


def lane_of_head(head, dim, lanes):
    lane = lax.broadcasted_iota(jnp.int32, (1, lanes), 1)
    return (lane >= head * dim) & (lane < (head + 1) * dim)


def only(values, lanes):
    return jnp.where(lanes, values, jnp.zeros_like(values))


def attend_kernel(scalars, packed, out, logs, *, rows, halo, dim):
    share = out.shape[1]
    first_end, second_end = scalars[1], scalars[2]
    edge_start, mid_start, edge_place, mid_place, halo_place = attention_places(scalars, rows, halo)
    half = rows // 2
    scale = 1.0 / math.sqrt(dim)
    mask_edge = edge_mask(edge_place, half, first_end, second_end)
    mask_mid, row_mid = mid_mask(mid_place, halo_place, halo, first_end, second_end)

    def one(queries, keys, values, mask):
        total, log_total = None, None
        for head in range(2):
            lanes = lane_of_head(head, dim, 128)
            scores = jnp.where(mask, over_features(only(queries, lanes), keys) * scale, MASKED)
            highest = jnp.max(scores, axis=-1, keepdims=True)
            raised = jnp.exp(scores - highest)
            sums = jnp.sum(raised, axis=-1, keepdims=True)
            weights = low(raised * (1.0 / sums))
            part = product(weights, only(values, lanes))
            total = part if total is None else total + part
            log_sum = highest + jnp.log(sums)
            log_total = log_sum if head == 0 else jnp.where(lanes, log_sum, log_total)
        return total, log_total

    def pair(index, carry):
        query_lanes = pl.ds(pl.multiple_of(index * 128, 128), 128)
        key_lanes = pl.ds(pl.multiple_of(share + index * 128, 128), 128)
        value_lanes = pl.ds(pl.multiple_of(2 * share + index * 128, 128), 128)
        edge = pl.ds(edge_start, half)
        mid = pl.ds(mid_start, halo)
        far = pl.ds(rows, halo)
        result, log_total = one(
            packed[edge, query_lanes], packed[edge, key_lanes], packed[edge, value_lanes], mask_edge
        )
        out[edge, query_lanes] = low(result)
        logs[edge, query_lanes] = log_total
        keys = jnp.concatenate([packed[mid, key_lanes], packed[far, key_lanes]], axis=0)
        values = jnp.concatenate([packed[mid, value_lanes], packed[far, value_lanes]], axis=0)
        result, log_total = one(packed[mid, query_lanes], keys, values, mask_mid)
        out[mid, query_lanes] = jnp.where(row_mid, low(result), out[mid, query_lanes])
        logs[mid, query_lanes] = jnp.where(row_mid, log_total, logs[mid, query_lanes])
        return carry

    lax.fori_loop(0, share // 128, pair, 0)


def attend_back_kernel(scalars, packed, grads, logs, out, *, rows, halo, dim):
    share = grads.shape[1]
    first_end, second_end = scalars[1], scalars[2]
    edge_start, mid_start, edge_place, mid_place, halo_place = attention_places(scalars, rows, halo)
    half = rows // 2
    scale = 1.0 / math.sqrt(dim)
    mask_edge = edge_mask(edge_place, half, first_end, second_end)
    mask_mid, _ = mid_mask(mid_place, halo_place, halo, first_end, second_end)

    def one(queries, keys, values, grad, log_total, mask):
        dquery, dkey, dvalue = None, None, None
        for head in range(2):
            lanes = lane_of_head(head, dim, 128)
            query, key, dout = only(queries, lanes), only(keys, lanes), only(grad, lanes)
            logs_here = log_total[:, head * dim : head * dim + 1]
            scores = jnp.where(mask, over_features(query, keys) * scale, MASKED)
            probs = jnp.exp(scores - logs_here)
            dprobs = over_features(dout, values)
            delta = jnp.sum(probs * dprobs, axis=-1, keepdims=True)
            dscores = low(probs * (dprobs - delta))
            parts = (
                product(dscores, key) * scale,
                over_rows(dscores, query) * scale,
                over_rows(low(probs), dout),
            )
            if head == 0:
                dquery, dkey, dvalue = parts
            else:
                dquery, dkey, dvalue = dquery + parts[0], dkey + parts[1], dvalue + parts[2]
        return low(dquery), low(dkey), low(dvalue)

    out[...] = jnp.zeros_like(out)

    def pair(index, carry):
        query_lanes = pl.ds(pl.multiple_of(index * 128, 128), 128)
        key_lanes = pl.ds(pl.multiple_of(share + index * 128, 128), 128)
        value_lanes = pl.ds(pl.multiple_of(2 * share + index * 128, 128), 128)
        edge = pl.ds(edge_start, half)
        mid = pl.ds(mid_start, halo)
        far = pl.ds(rows, halo)
        dquery, dkey, dvalue = one(
            packed[edge, query_lanes],
            packed[edge, key_lanes],
            packed[edge, value_lanes],
            grads[edge, query_lanes],
            logs[edge, query_lanes],
            mask_edge,
        )
        out[edge, query_lanes] = dquery
        out[edge, key_lanes] = dkey
        out[edge, value_lanes] = dvalue
        keys = jnp.concatenate([packed[mid, key_lanes], packed[far, key_lanes]], axis=0)
        values = jnp.concatenate([packed[mid, value_lanes], packed[far, value_lanes]], axis=0)
        dquery, dkey, dvalue = one(
            packed[mid, query_lanes],
            keys,
            values,
            grads[mid, query_lanes],
            logs[mid, query_lanes],
            mask_mid,
        )
        out[mid, query_lanes] = out[mid, query_lanes] + dquery
        out[mid, key_lanes] = out[mid, key_lanes] + dkey[:halo]
        out[mid, value_lanes] = out[mid, value_lanes] + dvalue[:halo]
        out[far, key_lanes] = dkey[halo:]
        out[far, value_lanes] = dvalue[halo:]
        return carry

    lax.fori_loop(0, share // 128, pair, 0)


def kernel_call(body, outs, operands, flops):
    return pl.pallas_call(
        body,
        out_shape=outs,
        in_specs=[pl.BlockSpec(memory_space=pltpu.SMEM)]
        + [pl.BlockSpec(memory_space=pltpu.VMEM)] * (len(operands) - 1),
        out_specs=[pl.BlockSpec(memory_space=pltpu.VMEM)] * len(outs),
        compiler_params=pltpu.CompilerParams(vmem_limit_bytes=48 * 1024 * 1024),
        cost_estimate=pl.CostEstimate(flops=flops, bytes_accessed=8_000_000, transcendentals=1_700_000),
    )(*operands)


def attend(scalars, packed, rows, halo, dim):
    share = packed.shape[1] // 3
    return kernel_call(
        functools.partial(attend_kernel, rows=rows, halo=halo, dim=dim),
        [jax.ShapeDtypeStruct((rows, share), LOWTYPE), jax.ShapeDtypeStruct((rows, share), WIDE)],
        [scalars, packed],
        1_700_000_000,
    )


def attend_back(scalars, packed, grads, logs, rows, halo, dim):
    [out] = kernel_call(
        functools.partial(attend_back_kernel, rows=rows, halo=halo, dim=dim),
        [jax.ShapeDtypeStruct(packed.shape, LOWTYPE)],
        [scalars, packed, grads, logs],
        4_000_000_000,
    )
    return out


def attention_grads_kernel(normed, dpacked, attended, dmerged, *refs):
    out, width = refs[-1], dmerged.shape[1]
    for i in range(3):
        part = over_rows(normed[...], dpacked[:, i * width : (i + 1) * width])
        out[:, i * width : (i + 1) * width] = low(part)
    out[:, 3 * width : 4 * width] = low(over_rows(attended[...], dmerged[...]))
    if len(refs) == 2:
        out[:, 4 * width :] = low(refs[0][...])


def attention_grads(*operands):
    normed, dpacked, _, dmerged = operands[:4]
    lanes = dpacked.shape[1] + dmerged.shape[1] + sum(o.shape[1] for o in operands[4:])
    inside = pl.BlockSpec(memory_space=pltpu.VMEM)
    return pl.pallas_call(
        attention_grads_kernel,
        out_shape=jax.ShapeDtypeStruct((normed.shape[1], lanes), LOWTYPE),
        in_specs=[inside] * len(operands),
        out_specs=inside,
        compiler_params=pltpu.CompilerParams(vmem_limit_bytes=40 * 1024 * 1024),
        cost_estimate=pl.CostEstimate(
            flops=2 * normed.shape[0] * normed.shape[1] * lanes,
            bytes_accessed=8_000_000,
            transcendentals=0,
        ),
    )(*operands)


def pick(block, index):
    return lax.dynamic_index_in_dim(block, index, 0, keepdims=False)


def xor_pairs(size, flip):
    return [(i, i ^ flip) for i in range(size)]


def assemble_kernel(coords, *refs, parts):
    blocks, outs = refs[: len(refs) - len(parts)], refs[len(refs) - len(parts) :]
    count = blocks[0].shape[0]
    for k, block in enumerate(blocks):
        chip = (coords[0] ^ (k >> 2)) * 4 + (coords[1] ^ ((k >> 1) & 1)) * 2 + (coords[2] ^ (k & 1))
        start = 0
        for out, (width, groups) in zip(outs, parts):
            for group in range(groups):
                place = pl.multiple_of((chip * groups + group) * count, 16)
                out[pl.ds(place, count), :] = block[:, start : start + width]
                start += width


def assemble(coords, blocks, parts):
    count, width = blocks[0].shape
    inside = pl.BlockSpec(memory_space=pltpu.VMEM)
    return pl.pallas_call(
        functools.partial(assemble_kernel, parts=parts),
        out_shape=[
            jax.ShapeDtypeStruct((len(blocks) * count * groups, lanes), LOWTYPE)
            for lanes, groups in parts
        ],
        in_specs=[pl.BlockSpec(memory_space=pltpu.SMEM)] + [inside] * len(blocks),
        out_specs=[inside] * len(parts),
        compiler_params=pltpu.CompilerParams(vmem_limit_bytes=40 * 1024 * 1024),
        cost_estimate=pl.CostEstimate(
            flops=0, bytes_accessed=4 * len(blocks) * count * width, transcendentals=0
        ),
    )(coords, *blocks)


def tie(*values):
    return lax.optimization_barrier(values)


def gather_z(pair, after=()):
    if lax.axis_size("z") != 4:
        return [lax.all_gather(pair, CHIPS, axis=0, tiled=True), pair]
    if after:
        pair, after = tie(pair, after)
    return [pair] + [lax.ppermute(pair, "z", xor_pairs(4, k)) for k in (1, 2, 3)]


def gather_plane(along):
    if lax.axis_size("z") != 4:
        return []
    return [(swap_chips(here), lax.ppermute(here, "y", SWAP)) for here in along]


def gather_end(along, plane, parts, x_first):
    if lax.axis_size("z") != 4:
        whole, count = along[0], along[1].shape[0]
        outs, start = [], 0
        for lanes, groups in parts:
            piece = whole[:, start : start + lanes * groups]
            piece = piece.reshape(-1, count, groups, lanes).transpose(0, 2, 1, 3)
            outs.append(piece.reshape(-1, lanes))
            start += lanes * groups
        return outs, ()
    blocks, across = [], []
    for k, (here, (by_x, by_y)) in enumerate(zip(along, plane)):
        if k in x_first:
            blocks += [here, by_x, by_y, lax.ppermute(by_x, "y", SWAP)]
            across += [by_x]
        else:
            blocks += [here, by_x, by_y, swap_chips(by_y)]
            across += [by_x, blocks[-1]]
    coords = jnp.stack([lax.axis_index(name) for name in CHIPS]).astype(jnp.int32)
    return assemble(coords, blocks, parts), tuple(across)


def added(left, right):
    return low(widen(left) + widen(right))


def at(values, index, axis):
    return lax.dynamic_index_in_dim(values, index, axis, keepdims=False)


def pairs_first(grads):
    if lax.axis_size("z") != 4:
        return lax.psum_scatter(low(grads), CHIPS, scatter_dimension=0, tiled=True)
    z, y, x = [lax.axis_index(name) for name in CHIPS]
    view = low(grads).reshape(2, 2, 2, 2, grads.shape[0] // 16, grads.shape[1])
    near, far = at(view, z // 2, 0), at(view, 1 - z // 2, 0)
    from_y, from_x = lax.ppermute(at(near, 1 - y, 1), "y", SWAP), swap_chips(at(far, 1 - x, 2))
    return at(near, y, 1), from_y, at(far, x, 2), from_x


def pairs_second(state):
    if lax.axis_size("z") != 4:
        return state
    y, x = lax.axis_index("y"), lax.axis_index("x")
    near, far = added(*state[:2]), added(*state[2:])
    from_x, from_y = swap_chips(at(near, 1 - x, 1)), lax.ppermute(at(far, 1 - y, 1), "y", SWAP)
    return at(near, x, 1), from_x, at(far, y, 1), from_y


def pairs_z(state):
    if lax.axis_size("z") != 4:
        return state
    low_bit = lax.axis_index("z") % 2
    near, far = added(*state[:2]), added(*state[2:])
    sent = (at(near, 1 - low_bit, 0), at(far, low_bit, 0), at(far, 1 - low_bit, 0))
    got = [lax.ppermute(piece, "z", xor_pairs(4, k + 1)) for k, piece in enumerate(sent)]
    return [at(near, low_bit, 0)] + got


def summed_everywhere(values):
    if lax.axis_size("z") != 4:
        return lax.psum(values, ALL)
    for name, pairs in (("c", SWAP), ("x", SWAP), ("y", SWAP), ("z", xor_pairs(4, 1)), ("z", xor_pairs(4, 2))):
        values = values + lax.ppermute(values, name, pairs)
    return values


def scatter_y(grads):
    if lax.axis_size("z") != 4:
        return lax.psum_scatter(low(grads), CHIPS, scatter_dimension=0, tiled=True)
    y = lax.axis_index("y")
    view = low(grads).reshape(4, 2, 2, grads.shape[0] // 16, grads.shape[1])
    return at(view, y, 1), lax.ppermute(at(view, 1 - y, 1), "y", SWAP)


def scatter_x(state):
    if lax.axis_size("z") != 4:
        return state
    x, values = lax.axis_index("x"), added(*state)
    return at(values, x, 1), swap_chips(at(values, 1 - x, 1))


def scatter_z(state):
    if lax.axis_size("z") != 4:
        return state
    z, values = lax.axis_index("z"), added(*state)
    sent = [lax.ppermute(at(values, z ^ k, 0), "z", xor_pairs(4, k)) for k in (1, 2, 3)]
    return [at(values, z, 0)] + sent


def scatter_end(state):
    if lax.axis_size("z") != 4:
        return widen(state)
    return widen(state[0]) + widen(state[1]) + widen(state[2]) + widen(state[3])


def exchange_halves(first, second, core):
    mine = jnp.where(core == 0, first, second)
    other = widen(swap_cores(low(jnp.where(core == 0, second, first))))
    return mine, other


def cut_kernel(place, weight, *outs):
    for k, out in enumerate(outs):

        @pl.when(pl.program_id(0) == k)
        def _(out=out):
            out[...] = low(weight[...])


def cut_columns(weight, place):
    rows, units = weight.shape[0], weight.shape[1] // 4
    return pl.pallas_call(
        cut_kernel,
        grid_spec=pltpu.PrefetchScalarGridSpec(
            num_scalar_prefetch=1,
            grid=(4,),
            in_specs=[pl.BlockSpec((rows, units), lambda i, p: (0, p[0] ^ i))],
            out_specs=[pl.BlockSpec((rows, units), lambda i, p: (0, 0))] * 4,
        ),
        out_shape=[jax.ShapeDtypeStruct((rows, units), LOWTYPE)] * 4,
        compiler_params=pltpu.CompilerParams(vmem_limit_bytes=32 * 1024 * 1024),
        cost_estimate=pl.CostEstimate(flops=0, bytes_accessed=6 * weight.size, transcendentals=0),
    )(place, weight)


def stack_kernel(place, *refs):
    blocks, out = refs[:4], refs[4]
    count = blocks[0].shape[0]
    for k, block in enumerate(blocks):
        out[pl.ds(pl.multiple_of((place[0] ^ k) * count, 16), count), :] = block[...]


def stack_rows(place, blocks):
    count, width = blocks[0].shape
    inside = pl.BlockSpec(memory_space=pltpu.VMEM)
    return pl.pallas_call(
        stack_kernel,
        out_shape=jax.ShapeDtypeStruct((4 * count, width), LOWTYPE),
        in_specs=[pl.BlockSpec(memory_space=pltpu.SMEM)] + [inside] * 4,
        out_specs=inside,
        compiler_params=pltpu.CompilerParams(vmem_limit_bytes=32 * 1024 * 1024),
        cost_estimate=pl.CostEstimate(flops=0, bytes_accessed=16 * count * width, transcendentals=0),
    )(place, *blocks)


def join_kernel(place, *refs):
    for k in range(4):

        @pl.when(pl.program_id(0) == k)
        def _(k=k):
            refs[4][...] = widen(refs[k][...])


def join_columns(place, pieces):
    rows, units = pieces[0].shape
    return pl.pallas_call(
        join_kernel,
        grid_spec=pltpu.PrefetchScalarGridSpec(
            num_scalar_prefetch=1,
            grid=(4,),
            in_specs=[pl.BlockSpec((rows, units), lambda i, p: (0, 0))] * 4,
            out_specs=pl.BlockSpec((rows, units), lambda i, p: (0, p[0] ^ i)),
        ),
        out_shape=jax.ShapeDtypeStruct((rows, 4 * units), WIDE),
        compiler_params=pltpu.CompilerParams(vmem_limit_bytes=40 * 1024 * 1024),
        cost_estimate=pl.CostEstimate(flops=0, bytes_accessed=24 * rows * units, transcendentals=0),
    )(place, *pieces)


def column_sums(values):
    return product(jnp.ones((8, values.shape[0]), LOWTYPE), values)[0]


def halves_of(weight, width):
    parts = [weight[:, i : i + width] for i in range(0, weight.shape[1], width)]
    return tuple(
        jnp.concatenate([p[:, h * width // 2 : (h + 1) * width // 2] for p in parts], axis=1)
        for h in range(2)
    )


def cut_dense(project, merge, small, expand, shrink, upper_project, upper_merge):
    width = merge.shape[1]
    half_rows = shrink.shape[0] // 2
    project, merge = halves_of(project, width), halves_of(merge, width)
    upper_project, upper_merge = halves_of(upper_project, width), halves_of(upper_merge, width)
    expand, shrink = halves_of(expand, expand.shape[1]), halves_of(shrink, width)
    return [
        (
            jnp.concatenate([project[h], merge[h], small], axis=1),
            jnp.concatenate([expand[h], upper_project[h], upper_merge[h]], axis=1),
            jnp.concatenate([shrink[h][:half_rows], shrink[h][half_rows:]], axis=1),
        )
        for h in range(2)
    ]


def prologue_kernel(core, *refs, count):
    operands = count + 9
    sources, outs = refs[:operands], refs[operands : operands + 6]
    table, small, sems = refs[operands + 6 : operands + 9]
    inside = refs[operands + 9 :]
    copies = [
        pltpu.make_async_copy(source, target, sems.at[i])
        for i, (source, target) in enumerate(zip(sources, inside))
    ]
    for copy in copies:
        copy.start()
    for copy in copies:
        copy.wait()
    vectors, (expand_bias, router, bias), weights = inside[:count], inside[count : count + 3], inside[count + 3 :]
    part = router.shape[0]
    table[...] = jnp.zeros_like(table)
    for i, vector in enumerate(vectors):
        table[i : i + 1, 0:part] = vector[...].reshape(1, part)
    biases = expand_bias[...].reshape(1, 4 * part)
    for q in range(4):
        table[16 + q : 17 + q, 0:part] = biases[:, q * part : (q + 1) * part]
    small[...] = table[...].T
    small[0:part, 32 : 32 + router.shape[1]] = router[...]
    small[0:part, 64 : 64 + bias.shape[1]] = bias[...]
    values = [ref[...] for ref in weights]
    cut = cut_dense(values[0], values[1], small[0:part, :], *values[2:])
    first = core[0] == 0
    for i in range(3):
        outs[i][...] = low(jnp.where(first, cut[0][i], cut[1][i]))
        outs[3 + i][...] = low(jnp.where(first, cut[1][i], cut[0][i]))


def prologue(core, vectors, expand_bias, router, bias, weights):
    part = router.shape[0]
    if lax.axis_size("z") != 4:
        rows = [jnp.stack(vectors), jnp.zeros((16 - len(vectors), part), WIDE)]
        rows += [expand_bias.reshape(4, part), jnp.zeros((12, part), WIDE)]
        small = jnp.concatenate([jnp.concatenate(rows).T, router, bias], axis=1)
        small = jnp.pad(small, ((0, 0), (0, 128 - small.shape[1])))
        cut = cut_dense(weights[0], weights[1], small, *weights[2:])
        picked = [[jnp.where(core == h, a, b) for a, b in zip(*cut)] for h in range(2)]
        return [low(v) for v in picked[0]], [low(v) for v in picked[1]]
    lanes = [weights[0].shape[1] // 2 + weights[1].shape[1] // 2 + 128]
    lanes += [sum(w.shape[1] // 2 for w in (weights[2], weights[4], weights[5]))]
    shapes = [(part, lanes[0]), (part, lanes[1]), (weights[3].shape[0] // 2, weights[3].shape[1])]
    inside = pl.BlockSpec(memory_space=pltpu.VMEM)
    operands = [*vectors, expand_bias, router, bias, *weights]
    outs = pl.pallas_call(
        functools.partial(prologue_kernel, count=len(vectors)),
        out_shape=[jax.ShapeDtypeStruct(shape, LOWTYPE) for shape in shapes * 2],
        in_specs=[pl.BlockSpec(memory_space=pltpu.SMEM)]
        + [pl.BlockSpec(memory_space=pl.ANY)] * len(operands),
        out_specs=[inside] * 6,
        scratch_shapes=[
            pltpu.VMEM((128, 128), WIDE),
            pltpu.VMEM((128, 128), WIDE),
            pltpu.SemaphoreType.DMA((len(operands),)),
        ]
        + [pltpu.VMEM(operand.shape, WIDE) for operand in operands],
        compiler_params=pltpu.CompilerParams(vmem_limit_bytes=60 * 1024 * 1024),
        cost_estimate=pl.CostEstimate(flops=0, bytes_accessed=2_500_000, transcendentals=0),
    )(core.reshape(1).astype(jnp.int32), *operands)
    return outs[:3], outs[3:]


def local(
    patches,
    image_lengths,
    expert_ids,
    lower_norm_gain,
    lower_norm_shift,
    lower_project,
    lower_query_bias,
    lower_value_bias,
    lower_merge,
    lower_merge_bias,
    lower_second_gain,
    lower_second_shift,
    lower_expand,
    lower_expand_bias,
    lower_shrink,
    lower_shrink_bias,
    upper_norm_gain,
    upper_norm_shift,
    upper_project,
    upper_query_bias,
    upper_value_bias,
    upper_merge,
    upper_merge_bias,
    upper_second_gain,
    upper_second_shift,
    router,
    expert_expand,
    expert_expand_bias,
    expert_shrink,
    expert_shrink_bias,
    output_grad,
):
    x, core = lax.axis_index("x"), lax.axis_index("c")
    devices = lax.axis_size(ALL)
    here = lax.axis_index(ALL)
    own, width = patches.shape
    rows = 2 * own
    dim = width // HEADS
    halo = rows - EDGE
    share = width // 2
    experts = router.shape[1]
    copies = devices // experts
    slots = experts * SLOTS
    part = lower_norm_gain.shape[0]
    lengths = image_lengths[0]
    scalars = jnp.stack([x, lengths[0], lengths[0] + lengths[1]]).astype(jnp.int32)
    mid_start = (1 - x) * (rows - halo)

    def halo_rows(full):
        count = halo // 2
        piece = lax.dynamic_slice_in_dim(full, mid_start + core * count, count, 0)
        got = swap_chips(piece)
        return in_order(got, swap_cores(got), core, 0)

    vectors = [
        lower_norm_gain,
        lower_norm_shift,
        lower_query_bias,
        lower_value_bias,
        lower_merge_bias,
        lower_second_gain,
        lower_second_shift,
        lower_shrink_bias,
        upper_norm_gain,
        upper_norm_shift,
        upper_query_bias,
        upper_value_bias,
        upper_merge_bias,
        upper_second_gain,
        upper_second_shift,
    ]
    count = len(vectors)
    shares, others = prologue(
        core,
        vectors,
        lower_expand_bias,
        router,
        expert_shrink_bias.T,
        [lower_project, lower_merge, lower_expand, lower_shrink, upper_project, upper_merge],
    )
    got = [swap_cores(other) for other in others]
    pair_1 = in_order(shares[0], got[0], core, 0)
    hidden_half = lower_expand.shape[1] // 2
    pair_2 = in_order(shares[1], got[1], core, 0)
    pair_3 = pair_2[:, hidden_half:]
    pair_2 = jnp.concatenate(
        [pair_2[:, :hidden_half], in_order(shares[2], got[2], core, 1)], axis=1
    )
    along_1 = gather_z(pair_1)
    (lower_project_c, lower_merge_c, table), _ = gather_end(
        along_1, gather_plane(along_1), ((3 * share, 1), (share, 1), (128, 1)), (0, 2)
    )
    seat = (2 * x + core).reshape(1).astype(jnp.int32)
    expand_cut, shrink_cut = cut_columns(expert_expand, seat), cut_columns(expert_shrink.T, seat)
    table, expand_cut, shrink_cut = lax.optimization_barrier((table, expand_cut, shrink_cut))
    along_2 = gather_z(pair_2, tuple(along_1[1:2]))
    (expand_c, shrink_half), crossed = gather_end(
        along_2, gather_plane(along_2), ((hidden_half, 1), (share, 4)), (0, 2)
    )
    upper_c = lax.all_gather(pair_3, CHIPS, axis=0, tiled=True)
    upper_project_c, upper_merge_c = upper_c[:, : 3 * share], upper_c[:, 3 * share :]
    lower_merge_full = in_order(lower_merge_c, swap_cores(lower_merge_c), core, 1)
    shrink_parts = shrink_half.reshape(2, hidden_half, share)
    shrink_c = in_order(pick(shrink_parts, core), swap_cores(pick(shrink_parts, 1 - core)), core, 1)
    table_t = table.T
    wide_t = widen(table_t[:32])
    (
        ln1_gain,
        ln1_shift,
        lower_qb,
        lower_vb,
        lower_mb,
        ln2_gain,
        ln2_shift,
        shrink_b,
        ln3_gain,
        ln3_shift,
        upper_qb,
        upper_vb,
        upper_mb,
        ln4_gain,
        ln4_shift,
    ) = [wide_t[i] for i in range(count)]
    expand_b = wide_t[16:20].reshape(4, devices, part).transpose(1, 0, 2).reshape(2, hidden_half)
    expand_b = pick(expand_b, core)
    router_w = table[:, 32 : 32 + experts]
    router_t = table_t[32 : 32 + experts]
    expert_bias = table_t[64 : 64 + experts]

    def between(values, k):
        return lax.ppermute(values, ("x", "c"), xor_pairs(4, k))

    def whole_expert(pieces):
        if crossed:
            pieces, _ = lax.optimization_barrier((pieces, crossed))
        across = between(pieces[2], 2)
        last, _ = tie(pieces[3], across)
        return [pieces[0], between(pieces[1], 1), across, between(last, 3)]

    def expert_parts(grads):
        count = grads.shape[0] // 4
        pieces = [
            lax.dynamic_slice_in_dim(grads, (seat[0] ^ k) * count, count, 0) for k in range(4)
        ]
        far_piece = between(pieces[2], 2)
        last, _ = tie(pieces[3], far_piece)
        return [pieces[0], between(pieces[1], 1), far_piece, between(last, 3)]

    expand_e = whole_expert(expand_cut)
    shrink_e = whole_expert(shrink_cut)

    order = lax.broadcasted_iota(jnp.int32, (own, own), 0)
    before_it = low(order > lax.broadcasted_iota(jnp.int32, (own, own), 1))
    chosen = [
        low(expert_ids[:, k : k + 1] == jnp.arange(experts, dtype=jnp.int32)[None]) for k in range(2)
    ]
    earlier = product(before_it, chosen[0] + chosen[1])
    places = [
        expert_ids[:, k] * SLOTS
        + jnp.sum(widen(chosen[k]) * earlier, axis=1).astype(jnp.int32)
        for k in range(2)
    ]
    placed = [
        low(place[:, None] == jnp.arange(slots, dtype=jnp.int32)[None]) for place in places
    ]
    placed_any = placed[0] + placed[1]

    def to_experts(values):
        sent = low(over_rows(placed_any, values)).reshape(experts, SLOTS, width)
        if copies > 1:
            sent = jnp.repeat(sent, copies, axis=0)
        got = lax.all_to_all(sent, ALL, 0, 0, tiled=True)
        return got.reshape(devices * SLOTS, width)

    def to_patches(values):
        got = lax.all_to_all(low(values).reshape(devices, SLOTS, width), ALL, 0, 0, tiled=True)
        if copies > 1:
            got = low(jnp.sum(widen(got.reshape(experts, copies, SLOTS, width)), axis=1))
        return got.reshape(slots, width)

    grads_sent = low(output_grad)

    full = in_order(patches, swap_cores(patches), core, 0)
    x0 = widen(full)

    def half(vector):
        return lax.dynamic_slice_in_dim(vector, core * share, share, 0)

    def attention_forward(residual, normed, project_c, query_bias, value_bias):
        bias = jnp.concatenate([half(query_bias), jnp.zeros((share,), WIDE), half(value_bias)])
        packed = low(product(normed, project_c) + bias)
        attended, logs = attend(scalars, packed, rows, halo, dim)
        attended_full = in_order(attended, swap_cores(attended), core, 1)
        return packed, logs, attended_full

    a1 = layer_norm(jnp.concatenate([x0, widen(halo_rows(full))], axis=0), ln1_gain, ln1_shift)
    packed1, logs1, attended1 = attention_forward(x0, a1, lower_project_c, lower_qb, lower_vb)
    x1 = x0 + product(attended1, lower_merge_full) + lower_mb

    b = layer_norm(x1, ln2_gain, ln2_shift)
    pre = product(b, expand_c) + expand_b
    hidden = low(gelu_parts(pre)[0])
    upper_merge_full = in_order(upper_merge_c, swap_cores(upper_merge_c), core, 1)
    hidden_full = in_order(hidden, swap_cores(hidden), core, 1)
    partial = low(product(hidden, shrink_c))
    x2 = x1 + (widen(partial) + widen(swap_cores(partial))) + shrink_b

    a2_own = layer_norm(x2, ln3_gain, ln3_shift)
    a2 = jnp.concatenate([a2_own, halo_rows(a2_own)], axis=0)
    a2, expand_e[2] = tie(a2, expand_e[2])
    packed2, logs2, attended2 = attention_forward(x2, a2, upper_project_c, upper_qb, upper_vb)

    attended2, expand_e[3], grad_rows = tie(attended2, expand_e[3], to_experts(grads_sent))

    def own_rows(values):
        return lax.dynamic_slice_in_dim(values, core * own, own, 0)

    x3 = own_rows(x2) + product(own_rows(attended2), upper_merge_full) + upper_mb
    normed = layer_norm(x3, ln4_gain, ln4_shift)
    rows_in = to_experts(normed)
    rows_in, expand_e, shrink_e[2] = tie(rows_in, expand_e, shrink_e[2])
    expand_e, shrink_e = stack_rows(seat, expand_e), stack_rows(seat, shrink_e)

    def gating(values):
        logits = product(values, router_w)
        raised = jnp.exp(logits - jnp.max(logits, axis=1, keepdims=True))
        return raised / jnp.sum(raised, axis=1, keepdims=True)

    mine = (jnp.arange(experts, dtype=jnp.int32) == here // copies).astype(WIDE)[None]
    probs_in = gating(rows_in)
    gate_in = jnp.sum(probs_in * mine, axis=1, keepdims=True)
    raw = product(grad_rows, shrink_e)
    before = product(rows_in, expand_e) + expert_expand_bias.astype(LOWTYPE).astype(WIDE)
    expert_hidden, slope = gelu_parts(before)
    expert_hidden = low(expert_hidden)
    once = (here % copies == 0).astype(WIDE)
    bias_here = product(low(mine), expert_bias) * once
    delta_gate = jnp.sum(widen(expert_hidden) * raw, axis=1, keepdims=True)
    delta_gate = delta_gate + jnp.sum(widen(grad_rows) * bias_here, axis=1, keepdims=True)
    dbefore = low(gate_in * raw * slope)
    dlogits = low(probs_in * delta_gate * (mine - gate_in))
    drows = over_features(dbefore, expand_e) + product(dlogits, router_t)
    drows, dbefore, expert_hidden = tie(low(drows), dbefore, expert_hidden)
    returned_grad = to_patches(drows)
    returned = to_patches(over_features(expert_hidden, shrink_e))
    g_out = low(gate_in * widen(grad_rows))
    delta_expand_e = over_rows(rows_in, dbefore)
    delta_shrink_e = over_rows(g_out, expert_hidden)
    delta_expert_bias = column_sums(dbefore)
    delta_router = over_rows(rows_in, dlogits)
    delta_shrink_e = low(delta_shrink_e)
    expand_pieces = expert_parts(low(delta_expand_e))
    returned_grad, expand_pieces[1], delta_shrink_e = tie(
        returned_grad, expand_pieces[1], delta_shrink_e
    )
    delta_shrink_bias = (column_sums(g_out) * once)[:, None] * mine

    delta_normed = product(placed_any, returned_grad)
    dx3, dgain4, dshift4 = layer_norm_back(x3, ln4_gain, delta_normed)
    dx3 = output_grad + dx3
    dx3 = in_order(dx3, swap_cores(dx3), core, 0)
    dx3, expand_pieces[2] = tie(dx3, expand_pieces[2])
    half_lanes = (jnp.arange(width, dtype=jnp.int32) // share == core).astype(WIDE)

    def columns_of_half(values):
        return lax.dynamic_slice_in_dim(values, core * share, share, 1)

    def spread(vector):
        return lax.dynamic_update_slice_in_dim(jnp.zeros((width,), WIDE), vector, core * share, 0)

    def attention_backward(
        dresidual, residual, normed, packed, logs, attended, gain, project_c, merge, waiting
    ):
        dmerged = low(dresidual)
        delta_merge_bias = column_sums(dmerged) * half_lanes
        merge_rows = lax.dynamic_slice_in_dim(merge, core * share, share, 0)
        dattended = low(over_features(dmerged, merge_rows))
        dpacked = attend_back(scalars, packed, dattended, logs, rows, halo, dim)
        dnormed = over_features(dpacked, project_c)
        dnormed, waiting = tie(dnormed, waiting)
        far = swap_chips(low(dnormed[rows:]))
        bias_sums = column_sums(dpacked)
        mine_part = low(
            dnormed[:rows]
            + lax.dynamic_update_slice_in_dim(jnp.zeros((rows, width), WIDE), widen(far), mid_start, 0)
        )
        dnormed = widen(mine_part) + widen(swap_cores(mine_part))
        dinput, dgain, dshift = layer_norm_back(residual, gain, dnormed)
        sums = (
            dgain * half_lanes,
            dshift * half_lanes,
            spread(bias_sums[:share]),
            spread(bias_sums[2 * share :]),
            delta_merge_bias,
        )
        outs = dresidual + dinput, (normed, dpacked, attended, columns_of_half(dmerged)), sums, far
        return *outs, waiting

    dx2, upper_grads, upper_sums, far, expand_pieces[3] = attention_backward(
        dx3,
        x2,
        a2,
        packed2,
        logs2,
        attended2,
        ln3_gain,
        upper_project_c,
        upper_merge_full,
        expand_pieces[3],
    )
    delta_shrink_e, _ = tie(delta_shrink_e, far)
    shrink_pieces = expert_parts(delta_shrink_e)
    third = scatter_y(attention_grads(*upper_grads))

    dmlp = low(dx2)
    delta_shrink_b = column_sums(dmlp) * half_lanes
    delta_shrink = low(over_rows(hidden_full, columns_of_half(dmlp)))
    delta_shrink = delta_shrink.reshape(-1, 4, 2 * part, share).transpose(0, 2, 1, 3)
    dpre = low(over_features(dmlp, shrink_c) * gelu_parts(pre)[1])
    dpre, shrink_pieces[2] = tie(dpre, shrink_pieces[2])
    dnormed = low(over_features(dpre, expand_c))
    delta_expand = low(over_rows(b, dpre))
    delta_expand_b = column_sums(dpre)
    second = pairs_first(
        jnp.concatenate([delta_expand, delta_shrink.reshape(width, 4 * share)], axis=1)
    )
    dinput, dgain2, dshift2 = layer_norm_back(x1, ln2_gain, widen(dnormed) + widen(swap_cores(dnormed)))
    dx1 = dx2 + dinput
    dx1, third, returned = tie(dx1, third, returned)
    third = scatter_x(third)

    dx0, lower_grads, lower_sums, _, (third, second) = attention_backward(
        dx1,
        x0,
        a1,
        packed1,
        logs1,
        attended1,
        ln1_gain,
        lower_project_c,
        lower_merge_full,
        (third, second),
    )
    second = pairs_second(second)
    third = scatter_z(third)
    dx0, returned = tie(dx0, returned)
    probs = gating(normed)
    result = x3
    for k in range(2):
        gate = jnp.sum(widen(chosen[k]) * probs, axis=1, keepdims=True)
        picked = product(placed[k], returned) + product(chosen[k], expert_bias)
        result = result + gate * picked

    delta_patches = own_rows(dx0)

    expand_sums = lax.dynamic_update_slice_in_dim(
        jnp.zeros((2 * hidden_half,), WIDE), delta_expand_b, core * hidden_half, 0
    )
    expand_sums = expand_sums.reshape(devices, 4, part).transpose(1, 0, 2).reshape(4, width)
    sums = jnp.concatenate(
        [
            jnp.stack(
                [jnp.zeros((width,), WIDE)] * 2
                + list(lower_sums[2:])
                + [dgain2 * half_lanes, dshift2 * half_lanes, delta_shrink_b]
                + list(upper_sums)
                + [dgain4, dshift4, jnp.zeros((width,), WIDE)]
            ),
            expand_sums,
            jnp.zeros((12, width), WIDE),
        ]
    )
    small_grads = jnp.concatenate([sums.T, delta_router, delta_shrink_bias], axis=1)
    small_grads = jnp.pad(small_grads, ((0, 0), (0, 128 - small_grads.shape[1])))
    first = pairs_first(attention_grads(*lower_grads, small_grads))
    first, third, expand_pieces, shrink_pieces = tie(first, third, expand_pieces, shrink_pieces)
    third = scatter_end(third)
    delta_expert_expand = join_columns(seat, expand_pieces)
    delta_expert_shrink = join_columns(seat, shrink_pieces)
    norm_sums = jnp.concatenate([jnp.stack(lower_sums[:2]), jnp.zeros((6, width), WIDE)])
    first, second, norm_sums, delta_expert_expand = tie(
        pairs_second(first), second, norm_sums, delta_expert_expand
    )
    first, second, norm_sums = pairs_z(first), pairs_z(second), summed_everywhere(norm_sums)
    first, second, norm_sums, delta_expert_shrink = tie(
        first, second, norm_sums, delta_expert_shrink
    )
    delta_expert_shrink = delta_expert_shrink.T
    first, second = scatter_end(first), scatter_end(second)
    norm_sums = lax.dynamic_slice_in_dim(norm_sums, here * part, part, 1)

    def attention_outputs(pair):
        mine, other = exchange_halves(pair[:part], pair[part:], core)
        both = [jnp.where(core == 0, mine, other), jnp.where(core == 0, other, mine)]
        cut = [[half[:, i * share : (i + 1) * share] for half in both] for i in range(4)]
        project = jnp.concatenate(cut[0] + cut[1] + cut[2], axis=1)
        return project, jnp.concatenate(cut[3], axis=1), mine[:, 4 * share :] + other[:, 4 * share :]

    delta_lower_project, delta_lower_merge, vector_grads = attention_outputs(first)
    delta_upper_project, delta_upper_merge, _ = attention_outputs(third)
    mine, other = exchange_halves(second[:part, :hidden_half], second[part:, :hidden_half], core)
    delta_lower_expand = in_order(mine, other, core, 1)
    mine, other = exchange_halves(
        second[:, hidden_half : hidden_half + width], second[:, hidden_half + width :], core
    )
    both = in_order(mine, other, core, 1)
    delta_lower_shrink = jnp.concatenate(
        [
            jnp.concatenate([both[:, i * share : (i + 1) * share] for i in (row, row + 2)], axis=1)
            for row in range(2)
        ],
        axis=0,
    )
    vector_t = vector_grads.T
    v = [norm_sums[0], norm_sums[1]] + [vector_t[i] for i in range(2, count)]
    delta_lower_expand_bias = vector_t[16:20].reshape(4 * part)
    delta_router_out = vector_grads[:, 32 : 32 + experts]
    delta_expert_shrink_bias = vector_t[64 : 64 + experts]
    return (
        result,
        delta_patches,
        v[0],
        v[1],
        delta_lower_project,
        v[2],
        v[3],
        delta_lower_merge,
        v[4],
        v[5],
        v[6],
        delta_lower_expand,
        delta_lower_expand_bias,
        delta_lower_shrink,
        v[7],
        v[8],
        v[9],
        delta_upper_project,
        v[10],
        v[11],
        delta_upper_merge,
        v[12],
        v[13],
        v[14],
        delta_router_out,
        delta_expert_expand,
        delta_expert_bias,
        delta_expert_shrink,
        delta_expert_shrink_bias,
    )


def solution(mesh):
    groups, parts = mesh.devices.shape
    inner = Mesh(mesh.devices.reshape(groups // 2, 2, parts // 2, 2), ALL)
    dp, seq = ("z", "y"), ("x", "c")
    rows, flat = P(ALL, None), P(ALL)
    in_specs = (
        (rows, P(dp, None), rows)
        + (flat, flat, rows, flat, flat, rows, flat)
        + (flat, flat, rows, flat, rows, flat)
        + (flat, flat, rows, flat, flat, rows, flat)
        + (flat, flat, rows, P(seq, dp), flat, P(dp, seq), P(None, ALL), rows)
    )
    out_specs = (
        (rows, rows)
        + (flat, flat, rows, flat, flat, rows, flat)
        + (flat, flat, rows, flat, rows, flat)
        + (flat, flat, rows, flat, flat, rows, flat)
        + (flat, flat, rows, P(seq, dp), flat, P(dp, seq), P(None, ALL))
    )
    return jax.shard_map(local, mesh=inner, in_specs=in_specs, out_specs=out_specs, check_vma=False)
```
